128 devices in a mesh: seq: 32 (over y_hi, x, z), tp: 4 (over y_lo, core).
Axes of the slice: x: 4, y: 4 (y_hi: 2, y_lo: 2; y = y_hi * 2 + y_lo), z: 4, core: 2. Of those that a mesh axis runs over, the one named last changes fastest.
Arguments:
- hidden_in: bfloat16 [8192, 4096], P('seq', 'tp'), may hold values from -6 to 6
- queries: bfloat16 [8192, 2048], P('seq', 'tp'), may hold values from -6 to 6
- keys: bfloat16 [8192, 2048], P('seq', 'tp'), may hold values from -6 to 6
- values: bfloat16 [8192, 2048], P('seq', 'tp'), may hold values from -6 to 6
- out_weight: bfloat16 [2048, 4096], P('tp'), may hold values from -0.125 to 0.125
- context_weight: bfloat16 [4096, 1024], P('tp'), may hold values from -0.1875 to 0.1875
- codes: int32 [8192, 4], P(('seq', 'tp')), may hold values from 0 to 1023
- table: bfloat16 [4, 1024, 1024], replicated, may hold values from -6 to 6
- depth_weights: bfloat16 [4, 1024, 1024], replicated, may hold values from -0.5 to 0.5
Outputs:
- losses: float32 [8192], P(('seq', 'tp'))
- grad_hidden: bfloat16 [8192, 4096], P('seq', 'tp')
The draws below stay inside these ranges and needn't reach their ends.
All inputs are finite; a program needn't handle non-finite values.
Results may differ from the reference program's by a relative error of at most 0.034.
Values may be sent and summed in bfloat16 or wider, within the bound.
No kernel may reach another device: no remote copies, remote signals or barrier semaphores. Data moves between devices by JAX's collectives and lax.ppermute only.
A program may use at most 192 MiB of HBM per device.

```python
import jax
import jax.numpy as jnp
from jax import lax

D = 4096
HEADS = 16
HD = 128
DD = 1024
DHEADS = 16
CB = 4
VOCAB = 1024
TOK_DEV = 256
FRAMES = 8192


def drawn_rows(key, count, width):
    return jnp.clip(jax.random.normal(jax.random.fold_in(key, 13), (count, width), jnp.float32), -6.0, 6.0)


def draw_queries(key, part):
    key = jax.random.fold_in(key, 1)
    filled = drawn_rows(key, FRAMES, HEADS * HD)
    return filled.astype(jnp.bfloat16)


def draw_keys(key, part):
    key = jax.random.fold_in(key, 2)
    filled = drawn_rows(key, FRAMES, HEADS * HD)
    return filled.astype(jnp.bfloat16)


def draw_table(key, part):
    key = jax.random.fold_in(key, 3)
    filled = drawn_rows(key, CB * VOCAB, DD).reshape(CB, VOCAB, DD)
    return filled.astype(jnp.bfloat16)


def draw_depth_weights(key, part):
    key = jax.random.fold_in(key, 4)
    stacked = jnp.clip(jax.random.normal(jax.random.fold_in(key, 25), (4, DD, DD), jnp.float32), -6.0, 6.0) / DD ** 0.5
    return stacked.astype(jnp.bfloat16)


def set_ends(result, rng, smallest, high):
    shape = result.shape
    index_at = [jax.random.randint(jax.random.fold_in(rng, axis), (), 0, shape[axis]) for axis in range(len(shape))]
    result = result.at[tuple(index_at)].set(smallest)
    longest = shape.index(max(shape))
    index_at[longest] = (index_at[longest] + 1) % shape[longest]
    return result.at[tuple(index_at)].set(high)


def shard_levels(key, shape, pieces, smallest, high):
    factor_of, own = 1.0, jax.random.fold_in(key, 6)
    for dim, blocks in pieces:
        steps = jnp.exp(jax.random.uniform(jax.random.fold_in(own, dim), (blocks,), jnp.float32, smallest / len(pieces), high / len(pieces)))
        factor_of = factor_of * jnp.repeat(steps, shape[dim] // blocks).reshape([-1 if axis == dim else 1 for axis in range(len(shape))])
    return factor_of


def bell_draw(own_key, extent, scale, most, shards=(), dtype=jnp.bfloat16):
    result = scale * jax.random.normal(own_key, extent, jnp.float32)
    if shards:
        result = result * shard_levels(own_key, extent, shards, -0.22, 0.18)
    return jnp.clip(result, -most, most).astype(dtype)


def setup_inputs(seed: int = 0) -> dict:
    key_list = jax.random.split(jax.random.key(seed), 10)
    hidden_in = bell_draw(key_list[0], (FRAMES, D), 1.0, 6.0, ((0, 32), (1, 4)))
    queries = draw_queries(jax.random.fold_in(key_list[9], 71), 0)
    keys = draw_keys(jax.random.fold_in(key_list[9], 71), 0)
    values = bell_draw(key_list[3], (FRAMES, HEADS * HD), 1.0, 6.0, ((0, 32), (1, 4)))
    out_weight = bell_draw(key_list[4], (HEADS * HD, D), (HEADS * HD) ** -0.5, 0.125, ((0, 4),))
    context_weight = bell_draw(key_list[5], (D, DD), (D // 4) ** -0.5, 0.1875, ((0, 4),))
    codes = set_ends(jax.random.randint(key_list[6], (FRAMES, CB), 0, VOCAB), jax.random.fold_in(key_list[6], 1), 0, VOCAB - 1).astype(jnp.int32)
    table = draw_table(jax.random.fold_in(key_list[9], 71), 0)
    depth_weights = draw_depth_weights(jax.random.fold_in(key_list[9], 71), 0)
    return {"hidden_in": hidden_in, "queries": queries, "keys": keys, "values": values, "out_weight": out_weight, "context_weight": context_weight, "codes": codes, "table": table, "depth_weights": depth_weights}


def normalize(stream):
    return stream * lax.rsqrt(lax.optimization_barrier(jnp.mean(stream * stream, -1, keepdims=True)) + 1e-05)

def depth_losses(context, codes, table, depth_weights):
    frames, width = context.shape
    books = table.shape[0]
    hsize = width // DHEADS
    earlier = [jnp.take(table[k], codes[:, k], axis=0) for k in range(books - 1)]
    shifted = jnp.stack([jnp.zeros((frames, width), jnp.bfloat16)] + earlier, 1).astype(jnp.float32)
    stream = context[:, None, :] + shifted
    normed = normalize(stream).astype(jnp.bfloat16).reshape(frames * books, width)
    query = jnp.dot(normed, depth_weights[0], preferred_element_type=jnp.float32).reshape(frames, books, DHEADS, hsize)
    key_part = jnp.dot(normed, depth_weights[1], preferred_element_type=jnp.float32).reshape(frames, books, DHEADS, hsize)
    value_part = jnp.dot(normed, depth_weights[2], preferred_element_type=jnp.float32).reshape(frames, books, DHEADS, hsize)
    scores = jnp.einsum('fqhd,fkhd->fhqk', query, key_part) / jnp.sqrt(jnp.float32(hsize))
    causal = jnp.arange(books)[:, None] >= jnp.arange(books)[None, :]
    scores = jnp.where(causal, scores, jnp.float32(-1e+30))
    weights = jax.nn.softmax(scores, -1)
    mixed = jnp.einsum('fhqk,fkhd->fqhd', weights, value_part).astype(jnp.bfloat16).reshape(frames * books, width)
    update = jnp.dot(mixed, depth_weights[3], preferred_element_type=jnp.float32).reshape(frames, books, width)
    final = normalize(stream + update).astype(jnp.bfloat16)
    total = jnp.zeros((frames,), jnp.float32)
    for k in range(books):
        logits = lax.dot_general(final[:, k, :], table[k], (((1,), (1,)), ((), ())), preferred_element_type=jnp.float32)
        logits = logits * (3.0 / jnp.sqrt(jnp.float32(width)))
        picked = jnp.take_along_axis(logits, codes[:, k:k + 1], axis=1)[:, 0]
        total = total + jax.nn.logsumexp(logits, -1) - picked
    return total

def reference(hidden_in, queries, keys, values, out_weight, context_weight, codes, table, depth_weights):
    frames = queries.shape[0]
    qh = queries.reshape(frames, HEADS, HD)
    kh = keys.reshape(frames, HEADS, HD).astype(jnp.float32)
    vh = values.reshape(frames, HEADS, HD).astype(jnp.float32)
    key_pos = jnp.arange(frames)

    def block(start):
        qb = lax.dynamic_slice_in_dim(qh, start, TOK_DEV, 0).astype(jnp.float32)
        scores = jnp.einsum('qhd,khd->hqk', qb, kh) / jnp.sqrt(jnp.float32(HD))
        qpos = start + jnp.arange(TOK_DEV)
        mask = key_pos[None, :] <= qpos[:, None]
        kept = jnp.where(mask[None], scores, jnp.float32(-1e+30))
        top = lax.optimization_barrier(jnp.max(kept, -1, keepdims=True))
        weight = jnp.where(mask[None], jnp.exp(scores - top), 0.0)
        total = lax.optimization_barrier(jnp.sum(weight, -1))
        summed = jnp.einsum('hqk,khd->qhd', weight.astype(jnp.bfloat16).astype(jnp.float32), vh)
        return (summed / total.T[:, :, None]).astype(jnp.bfloat16).reshape(TOK_DEV, HEADS * HD)
    starts = (jnp.arange(frames // TOK_DEV) * TOK_DEV).astype(jnp.int32)
    attended = lax.map(block, starts).reshape(frames, HEADS * HD)
    attn = jnp.dot(attended, out_weight, preferred_element_type=jnp.float32)
    hidden = (hidden_in.astype(jnp.float32) + attn).astype(jnp.bfloat16)
    context = jnp.dot(hidden, context_weight, preferred_element_type=jnp.float32)
    losses, pull = jax.vjp(lambda ctx: depth_losses(ctx, codes, table, depth_weights), context)
    dcontext = pull(jnp.ones_like(losses))[0].astype(jnp.bfloat16)
    grad_hidden = lax.dot_general(dcontext, context_weight, (((1,), (1,)), ((), ())), preferred_element_type=jnp.float32)
    return (losses, grad_hidden.astype(jnp.bfloat16))
```

```python
import functools
import itertools

import jax
import jax.numpy as jnp
from jax import lax
from jax.experimental import pallas as pl
from jax.experimental.pallas import tpu as pltpu
from jax.sharding import Mesh, PartitionSpec as P

HD = 128
DHEADS = 16
F32 = jnp.float32
BF16 = jnp.bfloat16
AXES = ("h", "x", "z", "l", "c")
SIZES = (2, 4, 4, 2, 2)
LOG2E = 1.4426950408889634
NEG = -1e30
VM = pl.BlockSpec(memory_space=pltpu.VMEM)
SM = pl.BlockSpec(memory_space=pltpu.SMEM)
ANY = pl.BlockSpec(memory_space=pl.ANY)


def flat(coords):
    number = 0
    for coord, size in zip(coords, SIZES):
        number = number * size + coord
    return number


def move(array, target):
    pairs = []
    for coords in itertools.product(*map(range, SIZES)):
        pairs.append((flat(coords), flat(target(*coords))))
    return lax.ppermute(array, AXES, pairs)


def other_core(h, x, z, l, c):
    return h, x, z, l, 1 - c


def x_up(h, x, z, l, c):
    return h, (x + 1) % 4, z, l, c


def x_down(h, x, z, l, c):
    return h, (x + 3) % 4, z, l, c


def z_by(n):
    return lambda h, x, z, l, c: (h, x, (z + n) % 4, l, c)


def l_swap(h, x, z, l, c):
    return h, x, z, 1 - l, c


def lc_swap(h, x, z, l, c):
    return h, x, z, 1 - l, 1 - c


def call(body, out_shape, in_specs, *args, scratch=(), limit=32, flops=0, nbytes=0, out_specs=None):
    if out_specs is None:
        out_specs = jax.tree.map(lambda _: VM, out_shape)
    return pl.pallas_call(
        body,
        out_shape=out_shape,
        in_specs=in_specs,
        out_specs=out_specs,
        scratch_shapes=list(scratch),
        compiler_params=pltpu.CompilerParams(vmem_limit_bytes=limit * 1024 * 1024),
        cost_estimate=pl.CostEstimate(flops=flops, bytes_accessed=nbytes, transcendentals=0),
    )(*args)


def shape(*dims, dtype=BF16):
    return jax.ShapeDtypeStruct(dims, dtype)


def dot_nn(a, b):
    return lax.dot_general(a, b, (((1,), (0,)), ((), ())), preferred_element_type=F32)


def dot_nt(a, b):
    return lax.dot_general(a, b, (((1,), (1,)), ((), ())), preferred_element_type=F32)


def dot_tn(a, b):
    return lax.dot_general(a, b, (((0,), (0,)), ((), ())), preferred_element_type=F32)


def split_rows_body(ids, q_ref, k_ref, v_ref, keep_ref, send_ref):
    c = ids[4]
    for part, ref in enumerate((q_ref, k_ref, v_ref)):
        for half in range(2):
            mine = pl.ds(pl.multiple_of(half * 128 + c * 64, 64), 64)
            theirs = pl.ds(pl.multiple_of(half * 128 + (1 - c) * 64, 64), 64)
            for head in range(4):
                cols = slice(head * 128, head * 128 + 128)
                keep_ref[c * 4 + head, half * 64 : half * 64 + 64, part * 128 : part * 128 + 128] = ref[mine, cols]
                send_ref[head, half * 64 : half * 64 + 64, part * 128 : part * 128 + 128] = ref[theirs, cols]


def attend(state, q, keys, vals, start, size, mask=None):
    acc_ref, m_ref, l_ref = state
    cols = slice(start, start + size)
    s = dot_nt(keys, q) * (LOG2E / HD**0.5)
    if mask is not None:
        s = jnp.where(mask, s, NEG)
    old = m_ref[:, cols]
    new = jnp.maximum(old, jnp.max(s, 0, keepdims=True))
    p = jnp.exp2(s - new)
    alpha = jnp.exp2(old - new)
    m_ref[:, cols] = new
    l_ref[:, cols] = l_ref[:, cols] * alpha + jnp.sum(p, 0, keepdims=True)
    acc_ref[:, cols] = acc_ref[:, cols] * alpha + dot_tn(vals, p.astype(BF16))


def rows_of(ref, first, count, col):
    return ref[first : first + count, :, col : col + 128].reshape(count * 128, 128)


def own_block_body(ids, r_ref, other_ref, acc_ref, m_ref, l_ref):
    state = (acc_ref, m_ref, l_ref)
    c = ids[4]
    m_ref[...] = jnp.full_like(m_ref, NEG)
    l_ref[...] = jnp.zeros_like(l_ref)
    acc_ref[...] = jnp.zeros_like(acc_ref)
    key_row = lax.broadcasted_iota(jnp.int32, (256, 128), 0)
    q_row = lax.broadcasted_iota(jnp.int32, (256, 128), 1)
    key_core = jnp.where(key_row < 128, c, 1 - c)
    key_row = key_row % 128
    place = lambda row, core: (row // 64) * 128 + core * 64 + row % 64
    mask = place(key_row, key_core) <= place(q_row, c)
    for h in range(2):
        for z in range(4):
            at = h * 4 + z
            keys = jnp.concatenate([r_ref[at, :, 128:256], other_ref[at, :, 0:128]], 0)
            vals = jnp.concatenate([r_ref[at, :, 256:384], other_ref[at, :, 128:256]], 0)
            attend(state, r_ref[at, :, 0:128], keys, vals, at * 128, 128, mask)
            if z < 3:
                q = rows_of(r_ref, at + 1, 3 - z, 0)
                attend(state, q, keys, vals, at * 128 + 128, (3 - z) * 128)
    q = rows_of(r_ref, 4, 4, 0)
    attend(state, q, rows_of(r_ref, 0, 4, 128), rows_of(r_ref, 0, 4, 256), 512, 512)
    attend(state, q, rows_of(other_ref, 0, 4, 0), rows_of(other_ref, 0, 4, 128), 512, 512)


def block_steps(state, r_ref, low, high, earlier):
    q1 = lambda: rows_of(r_ref, 4, 4, 0)
    for ref, at in low:
        attend(state, q1(), rows_of(ref, at, 4, 0), rows_of(ref, at, 4, 128), 512, 512)

    @pl.when(earlier)
    def _():
        for ref, at in low:
            attend(state, rows_of(r_ref, 0, 4, 0), rows_of(ref, at, 4, 0), rows_of(ref, at, 4, 128), 0, 512)
        for ref, at in high:
            attend(state, q1(), rows_of(ref, at, 4, 0), rows_of(ref, at, 4, 128), 512, 512)


def near_blocks_body(ids, r_ref, up, up_o, down, down_o, acc_in, m_in, l_in, acc_ref, m_ref, l_ref):
    acc_ref[...] = acc_in[...]
    m_ref[...] = m_in[...]
    l_ref[...] = l_in[...]
    state = (acc_ref, m_ref, l_ref)
    x = ids[1]
    block_steps(state, r_ref, [(up, 0), (up_o, 0)], [(up, 4), (up_o, 4)], x > 0)
    block_steps(state, r_ref, [(down, 0), (down_o, 0)], [(down, 4), (down_o, 4)], x == 3)


def far_block_body(ids, r_ref, lo, lo_o, hi, hi_o, acc_in, m_in, l_in, out_ref, acc_ref, m_ref, l_ref):
    acc_ref[...] = acc_in[...]
    m_ref[...] = m_in[...]
    l_ref[...] = l_in[...]
    state = (acc_ref, m_ref, l_ref)
    block_steps(state, r_ref, [(lo, 0), (lo_o, 0)], [(hi, 0), (hi_o, 0)], ids[1] >= 2)
    done = acc_ref[...] / l_ref[...]
    out_ref[...] = done.T.astype(BF16).reshape(8, 128, 128)


def merged_weight_body(ids, ow_ref, b00, b01, b10, b11, out_ref):
    l, c = ids[3], ids[4]
    total = None
    for dl, dc, ref in ((0, 0, b00), (0, 1, b01), (1, 0, b10), (1, 1, b11)):
        t = jnp.where(dl == 1, 1 - l, l) * 2 + jnp.where(dc == 1, 1 - c, c)
        part = dot_nn(ow_ref[:, pl.ds(pl.multiple_of(t * 1024, 1024), 1024)], ref[...])
        total = part if total is None else total + part
    out_ref[...] = total.astype(BF16)


def hidden_part_body(ids, hid_ref, cw_ref, own_ref, c_ref, l_ref, lc_ref):
    l, c = ids[3], ids[4]
    part = dot_nn(hid_ref[...], cw_ref[...])
    for t in range(4):
        piece = part[t * 64 : t * 64 + 64]
        same_l = l == t // 2
        same_c = c == t % 2

        @pl.when(same_l & same_c)
        def _():
            own_ref[...] = piece

        @pl.when(same_l & (~same_c))
        def _():
            c_ref[...] = piece.astype(BF16)

        @pl.when((~same_l) & same_c)
        def _():
            l_ref[...] = piece.astype(BF16)

        @pl.when((~same_l) & (~same_c))
        def _():
            lc_ref[...] = piece.astype(BF16)


def project_body(ids, att_ref, w_ref, wo_ref, own_ref, send_ref, out):
    z, l, c = ids[2], ids[3], ids[4]
    a_own = att_ref[pl.ds(c * 4, 4)]
    a_oth = att_ref[pl.ds((1 - c) * 4, 4)]
    a_own = jnp.concatenate([a_own[i] for i in range(4)], 1)
    a_oth = jnp.concatenate([a_oth[i] for i in range(4)], 1)
    for dz in range(4):
        col = pl.multiple_of(((z + 4 - dz) % 4) * 256, 256)
        out[:, pl.ds(col, 256)] = dot_nn(a_own, w_ref[dz]) + dot_nn(a_oth, wo_ref[dz])
    own_ref[...] = out[pl.ds(pl.multiple_of(l * 64, 64), 64), :]
    send_ref[...] = out[pl.ds(pl.multiple_of((1 - l) * 64, 64), 64), :].astype(BF16)


def rms(stream):
    return lax.rsqrt(jnp.mean(stream * stream, -1, keepdims=True) + 1e-05)


def split_dot(a, b):
    high = a.astype(BF16)
    low = (a - high.astype(F32)).astype(BF16)
    return dot_nn(high, b) + dot_nn(low, b)


def depth_body(
    att_ref, recv_ref, h0_ref, h1_ref, h2_ref, h3_ref, e1_ref, e2_ref, e3_ref, codes_ref, wt_hbm, tab_hbm,
    loss_ref, dctx_ref, wt, tab, sems,
):
    copies = [pltpu.make_async_copy(wt_hbm.at[i], wt.at[i], sems.at[i]) for i in range(4)]
    copies += [pltpu.make_async_copy(tab_hbm.at[i], tab.at[i], sems.at[4 + i]) for i in range(4)]
    for copy in copies:
        copy.start()
    n = 64
    context = att_ref[...] + recv_ref[...].astype(F32) + h0_ref[...]
    context = context + h1_ref[...].astype(F32) + h2_ref[...].astype(F32) + h3_ref[...].astype(F32)
    stream = jnp.concatenate([context] + [context + e[...].astype(F32) for e in (e1_ref, e2_ref, e3_ref)], 0)
    r1 = rms(stream)
    normed = (stream * r1).astype(BF16)
    qkv = []
    for i in range(3):
        copies[i].wait()
        qkv.append(dot_nn(normed, wt[i]))
    q, k, v = qkv
    at = lambda a, i: a[i * n : (i + 1) * n]
    pairs = [(i, j) for i in range(4) for j in range(i + 1)]
    lane = lax.broadcasted_iota(jnp.int32, (1024, 128), 0) // 64
    head = lax.broadcasted_iota(jnp.int32, (1024, 128), 1)
    gather_heads = (lane == head).astype(BF16)
    head_t = lax.broadcasted_iota(jnp.int32, (128, 1024), 0)
    lane_t = lax.broadcasted_iota(jnp.int32, (128, 1024), 1) // 64
    spread_heads = (lane_t == head_t).astype(BF16)
    prod = jnp.concatenate([at(q, i) * at(k, j) for i, j in pairs], 0)
    scores = split_dot(prod, gather_heads) * 0.125
    score = {pair: at(scores, number) for number, pair in enumerate(pairs)}
    weight = {}
    for i in range(4):
        top = functools.reduce(jnp.maximum, [score[i, j] for j in range(i + 1)])
        es = [jnp.exp(score[i, j] - top) for j in range(i + 1)]
        total = functools.reduce(jnp.add, es)
        for j in range(i + 1):
            weight[i, j] = es[j] / total
    spread = dot_nn(jnp.concatenate([weight[p] for p in pairs], 0).astype(BF16), spread_heads)
    wide = {pair: at(spread, number) for number, pair in enumerate(pairs)}
    mixed = jnp.concatenate(
        [functools.reduce(jnp.add, [wide[i, j] * at(v, j) for j in range(i + 1)]) for i in range(4)], 0
    ).astype(BF16)
    copies[3].wait()
    update = dot_nn(mixed, wt[3])
    out = stream + update
    r2 = rms(out)
    final = (out * r2).astype(BF16)
    loss = jnp.zeros((n, 1), F32)
    dfinal = []
    scale = 3.0 / 1024**0.5
    vocab = lax.broadcasted_iota(jnp.int32, (n, 1024), 1)
    for i in range(4):
        copies[4 + i].wait()
        logits = dot_nt(at(final, i), tab[i]) * scale
        top = jnp.max(logits, -1, keepdims=True)
        e = jnp.exp(logits - top)
        total = jnp.sum(e, -1, keepdims=True)
        hit = vocab == codes_ref[:, i : i + 1]
        picked = jnp.sum(jnp.where(hit, logits, 0.0), -1, keepdims=True)
        loss = loss + top + jnp.log(total) - picked
        dlogits = (e / total - hit.astype(F32)).astype(BF16)
        dfinal.append(dot_nn(dlogits, tab[i]) * scale)
    loss_ref[...] = jnp.broadcast_to(loss, (n, 128))
    dfinal = jnp.concatenate(dfinal, 0)
    dout = r2 * (dfinal - out * (r2 * r2) * jnp.mean(dfinal * out, -1, keepdims=True))
    dmixed = dot_nt(dout.astype(BF16), wt[3])
    dprod = jnp.concatenate([at(dmixed, i) * at(v, j) for i, j in pairs], 0)
    dweights = split_dot(dprod, gather_heads)
    dweight = {pair: at(dweights, number) for number, pair in enumerate(pairs)}
    dscore = []
    for i in range(4):
        mean = functools.reduce(jnp.add, [weight[i, j] * dweight[i, j] for j in range(i + 1)])
        for j in range(i + 1):
            dscore.append(weight[i, j] * (dweight[i, j] - mean) * 0.125)
    spread = dot_nn(jnp.concatenate(dscore, 0).astype(BF16), spread_heads)
    dwide = {pair: at(spread, number) for number, pair in enumerate(pairs)}
    add = lambda terms: functools.reduce(jnp.add, terms)
    dq = jnp.concatenate([add([dwide[i, j] * at(k, j) for j in range(i + 1)]) for i in range(4)], 0)
    dk = jnp.concatenate([add([dwide[i, j] * at(q, i) for i in range(j, 4)]) for j in range(4)], 0)
    dv = jnp.concatenate([add([wide[i, j] * at(dmixed, i) for i in range(j, 4)]) for j in range(4)], 0)
    dnormed = dot_nt(dq.astype(BF16), wt[0]) + dot_nt(dk.astype(BF16), wt[1]) + dot_nt(dv.astype(BF16), wt[2])
    dstream = dout + r1 * (dnormed - stream * (r1 * r1) * jnp.mean(dnormed * stream, -1, keepdims=True))
    dctx_ref[...] = add([at(dstream, i) for i in range(4)]).astype(BF16)


def grad_body(ids, d0, d1, d2, d3, cw_ref, out_ref, rows):
    l, c = ids[3], ids[4]
    for dl, dc, ref in ((0, 0, d0), (0, 1, d1), (1, 0, d2), (1, 1, d3)):
        t = jnp.where(dl == 1, 1 - l, l) * 2 + jnp.where(dc == 1, 1 - c, c)
        rows[pl.ds(pl.multiple_of(t * 64, 64), 64), :] = ref[...]
    out_ref[...] = dot_nt(rows[...], cw_ref[...]).astype(BF16)


def per_device(hidden_in, queries, keys, values, out_weight, context_weight, codes, table, depth_weights):
    coords = [lax.axis_index(name) for name in AXES]
    h, x, z, l, c = coords
    ids = jnp.stack(coords).astype(jnp.int32)

    keep, send = call(
        split_rows_body, (shape(8, 128, 384), shape(4, 128, 384)), [SM] + [VM] * 3, ids, queries, keys, values,
        nbytes=3 << 19,
    )
    full = lax.dynamic_update_slice(keep, move(send, other_core), ((1 - c) * 4, 0, 0))
    mine = lax.all_to_all(full, ("h", "z"), 0, 0, tiled=True)
    kv = mine[:, :, 128:384]

    up = move(kv, x_up)
    down = move(kv, x_down)
    kv_o = move(kv, other_core)

    stats = (shape(128, 1024, dtype=F32), shape(1, 1024, dtype=F32), shape(1, 1024, dtype=F32))
    carry = call(own_block_body, stats, [SM] + [VM] * 2, ids, mine, kv_o, flops=1 << 29, nbytes=2 << 20)

    cw_cols = lax.dynamic_slice_in_dim(context_weight, z * 256, 256, 1)
    cw_c = move(cw_cols, other_core)
    cw_l = move(cw_cols, l_swap)
    cw_lc = move(cw_l, other_core)
    merged = call(
        merged_weight_body, shape(512, 256), [SM] + [VM] * 5, ids, out_weight, cw_cols, cw_c, cw_l, cw_lc,
        flops=1 << 30, nbytes=6 << 20,
    )
    merged = jnp.stack([merged] + [move(merged, z_by(n)) for n in (1, 2, 3)])
    merged_o = move(merged, other_core)

    h_own, h_c, h_l, h_lc = call(
        hidden_part_body,
        (shape(64, 1024, dtype=F32), shape(64, 1024), shape(64, 1024), shape(64, 1024)),
        [SM] + [VM] * 2, ids, hidden_in, context_weight, flops=1 << 29, nbytes=3 << 20,
    )
    h_c, h_l, h_lc = move(h_c, other_core), move(h_l, l_swap), move(h_lc, lc_swap)
    earlier = [jnp.take(table[n], codes[:, n], axis=0, mode="clip") for n in range(3)]

    up_o = move(up, other_core)
    down_o = move(down, other_core)
    lo = move(up[:4], x_up)
    hi = move(down[4:], x_down)
    carry = call(
        near_blocks_body, stats, [SM] + [VM] * 8, ids, mine, up, up_o, down, down_o, *carry,
        flops=1 << 30, nbytes=4 << 20,
    )
    lo_o = move(lo, other_core)
    hi_o = move(hi, other_core)
    attended = call(
        far_block_body, shape(8, 128, 128), [SM] + [VM] * 8, ids, mine, lo, lo_o, hi, hi_o, *carry,
        scratch=[pltpu.VMEM(s.shape, s.dtype) for s in stats], flops=1 << 29, nbytes=3 << 20,
    )
    attended = lax.all_to_all(attended, ("h", "z"), 0, 0, tiled=True)

    own, send = call(
        project_body, (shape(64, 1024, dtype=F32), shape(64, 1024)), [SM] + [VM] * 3, ids, attended, merged, merged_o,
        scratch=[pltpu.VMEM((128, 1024), F32)], flops=1 << 28, nbytes=3 << 20,
    )
    recv = move(send, l_swap)
    losses, dcontext = call(
        depth_body, (shape(64, 128, dtype=F32), shape(64, 1024)), [VM] * 10 + [ANY] * 2,
        own, recv, h_own, h_c, h_l, h_lc, *earlier, codes, depth_weights, table,
        scratch=[pltpu.VMEM((4, 1024, 1024), BF16), pltpu.VMEM((4, 1024, 1024), BF16), pltpu.SemaphoreType.DMA((8,))],
        limit=56, flops=5 << 30, nbytes=17 << 20,
    )
    grad = call(
        grad_body, shape(256, 1024), [SM] + [VM] * 5, ids,
        dcontext, move(dcontext, other_core), move(dcontext, l_swap), move(dcontext, lc_swap), context_weight,
        scratch=[pltpu.VMEM((256, 1024), BF16)], flops=1 << 29, nbytes=3 << 20,
    )
    return losses[:, 0], grad


def solution(mesh):
    fine = Mesh(mesh.devices.reshape(SIZES), AXES)
    seq, tp = AXES[:3], AXES[3:]
    return jax.shard_map(
        per_device,
        mesh=fine,
        in_specs=(
            P(seq, tp), P(seq, tp), P(seq, tp), P(seq, tp), P(tp, None), P(tp, None), P(seq + tp, None), P(), P(),
        ),
        out_specs=(P(seq + tp), P(seq, tp)),
        check_vma=False,
    )
```

```python
import functools
import itertools

import jax
import jax.numpy as jnp
from jax import lax
from jax.experimental import pallas as pl
from jax.experimental.pallas import tpu as pltpu
from jax.sharding import Mesh, PartitionSpec as P

HD = 128
DHEADS = 16
F32 = jnp.float32
BF16 = jnp.bfloat16
AXES = ("h", "x", "z", "l", "c")
SIZES = (2, 4, 4, 2, 2)
LOG2E = 1.4426950408889634
NEG = -1e30
VM = pl.BlockSpec(memory_space=pltpu.VMEM)
SM = pl.BlockSpec(memory_space=pltpu.SMEM)
ANY = pl.BlockSpec(memory_space=pl.ANY)


def flat(coords):
    number = 0
    for coord, size in zip(coords, SIZES):
        number = number * size + coord
    return number


def move(array, target):
    pairs = []
    for coords in itertools.product(*map(range, SIZES)):
        pairs.append((flat(coords), flat(target(*coords))))
    return lax.ppermute(array, AXES, pairs)


def other_core(h, x, z, l, c):
    return h, x, z, l, 1 - c


def x_up(h, x, z, l, c):
    return h, (x + 1) % 4, z, l, c


def z_by(n):
    return lambda h, x, z, l, c: (h, x, (z + n) % 4, l, c)


def x_down(h, x, z, l, c):
    return h, (x + 3) % 4, z, l, c


def l_swap(h, x, z, l, c):
    return h, x, z, 1 - l, c


def lc_swap(h, x, z, l, c):
    return h, x, z, 1 - l, 1 - c


def call(body, out_shape, in_specs, *args, after=(), scratch=(), limit=16, flops=0, nbytes=0, aliases=None, out_specs=None):
    if out_specs is None:
        out_specs = jax.tree.map(lambda _: VM, out_shape)
    reads = len(args)

    def run(*refs):
        body(*refs[:reads], *refs[reads + len(after) :])

    args = args + tuple(after)
    in_specs = in_specs + [ANY] * len(after)
    return pl.pallas_call(
        run,
        out_shape=out_shape,
        in_specs=in_specs,
        out_specs=out_specs,
        scratch_shapes=list(scratch),
        input_output_aliases=aliases or {},
        compiler_params=pltpu.CompilerParams(vmem_limit_bytes=limit * 1024 * 1024),
        cost_estimate=pl.CostEstimate(flops=flops, bytes_accessed=nbytes, transcendentals=0),
    )(*args)


def shape(*dims, dtype=BF16):
    return jax.ShapeDtypeStruct(dims, dtype)


def dot_nn(a, b):
    return lax.dot_general(a, b, (((1,), (0,)), ((), ())), preferred_element_type=F32)


def dot_nt(a, b):
    return lax.dot_general(a, b, (((1,), (1,)), ((), ())), preferred_element_type=F32)


def dot_tn(a, b):
    return lax.dot_general(a, b, (((0,), (0,)), ((), ())), preferred_element_type=F32)


def split_rows_body(ids, q_hbm, k_hbm, v_hbm, w_hbm, keep_ref, send_ref, cols_ref, local, sems):
    c = ids[4]
    copies = [pltpu.make_async_copy(ref, local.at[n], sems.at[n]) for n, ref in enumerate((q_hbm, k_hbm, v_hbm))]
    cols = pl.ds(pl.multiple_of(ids[2] * 256, 256), 256)
    copies.append(pltpu.make_async_copy(w_hbm.at[:, cols], cols_ref, sems.at[3]))
    for copy in copies:
        copy.start()
    for part in range(3):
        copies[part].wait()
        for half in range(2):
            mine = pl.ds(pl.multiple_of(half * 128 + c * 64, 64), 64)
            theirs = pl.ds(pl.multiple_of(half * 128 + (1 - c) * 64, 64), 64)
            for head in range(4):
                cols = slice(head * 128, head * 128 + 128)
                to = slice(part * 128, part * 128 + 128)
                keep_ref[c * 4 + head, half * 64 : half * 64 + 64, to] = local[part, mine, cols]
                send_ref[head, half * 64 : half * 64 + 64, to] = local[part, theirs, cols]
    copies[3].wait()


def attend(state, q, keys, vals, start, mask=None):
    acc_ref, m_ref, l_ref = state
    cols = slice(start, start + 512)
    s = dot_nt(keys, q) * (LOG2E / HD**0.5)
    if mask is not None:
        s = jnp.where(mask, s, NEG)
    old = m_ref[:, cols]
    new = jnp.maximum(old, jnp.max(s, 0, keepdims=True))
    p = jnp.exp2(s - new)
    alpha = jnp.exp2(old - new)
    m_ref[:, cols] = new
    l_ref[:, cols] = l_ref[:, cols] * alpha + jnp.sum(p, 0, keepdims=True)
    acc_ref[:, cols] = acc_ref[:, cols] * alpha + dot_tn(vals, p.astype(BF16))


def rows_of(ref, first, col):
    return ref[first : first + 4, :, col : col + 128].reshape(512, 128)


def take_rows_body(r_ref, lo_ref, hi_ref, q_ref):
    q_ref[...] = r_ref[:, :, 0:128]
    lo_ref[...] = r_ref[0:4, :, 128:384]
    hi_ref[...] = r_ref[4:8, :, 128:384]


def own_block_body(ids, q_ref, q_o_ref, lo_ref, hi_ref, acc_ref, m_ref, l_ref):
    state = (acc_ref, m_ref, l_ref)
    c = ids[4]
    m_ref[...] = jnp.full_like(m_ref, 0.1 * NEG)
    l_ref[...] = jnp.zeros_like(l_ref)
    acc_ref[...] = jnp.zeros_like(acc_ref)
    key_row = lax.broadcasted_iota(jnp.int32, (512, 512), 0)
    q_row = lax.broadcasted_iota(jnp.int32, (512, 512), 1)
    place = lambda row, core: (row // 64) * 128 + core * 64 + row % 64
    key_place = place(key_row, c)
    for section, (ref, core) in enumerate(((q_ref, c), (q_o_ref, 1 - c))):
        mask = key_place <= place(q_row, core)
        for h, kv in enumerate((lo_ref, hi_ref)):
            q = rows_of(ref, h * 4, 0)
            attend(state, q, rows_of(kv, 0, 0), rows_of(kv, 0, 128), h * 1024 + section * 512, mask)
        attend(state, q, rows_of(lo_ref, 0, 0), rows_of(lo_ref, 0, 128), 1024 + section * 512)


def block_steps(state, qs, low, high, earlier):
    for section, ref in enumerate(qs):
        attend(state, rows_of(ref, 4, 0), rows_of(low, 0, 0), rows_of(low, 0, 128), 1024 + section * 512)

    @pl.when(earlier)
    def _():
        for section, ref in enumerate(qs):
            attend(state, rows_of(ref, 0, 0), rows_of(low, 0, 0), rows_of(low, 0, 128), section * 512)
            attend(state, rows_of(ref, 4, 0), rows_of(high, 0, 0), rows_of(high, 0, 128), 1024 + section * 512)


def near_blocks_body(
    ids, q_ref, q_o_ref, up_lo, up_hi, down_lo, down_hi, acc_in, m_in, l_in, acc_ref, m_ref, l_ref
):
    acc_ref[...] = acc_in[...]
    m_ref[...] = m_in[...]
    l_ref[...] = l_in[...]
    state = (acc_ref, m_ref, l_ref)
    x = ids[1]
    block_steps(state, (q_ref, q_o_ref), up_lo, up_hi, x > 0)
    block_steps(state, (q_ref, q_o_ref), down_lo, down_hi, x == 3)


def far_block_body(ids, q_ref, q_o_ref, lo, hi, acc_in, m_in, l_in, own_ref, send_ref, own_stat, send_stat, acc_ref, m_ref, l_ref):
    acc_ref[...] = acc_in[...]
    m_ref[...] = m_in[...]
    l_ref[...] = l_in[...]
    state = (acc_ref, m_ref, l_ref)
    block_steps(state, (q_ref, q_o_ref), lo, hi, ids[1] >= 2)
    for section, (ref, stat) in enumerate(((own_ref, own_stat), (send_ref, send_stat))):
        for h in range(2):
            cols = slice(h * 1024 + section * 512, h * 1024 + section * 512 + 512)
            to = slice(h * 512, h * 512 + 512)
            total = l_ref[:, cols]
            ref[:, to] = (acc_ref[:, cols] / jnp.maximum(total, 0.5)).astype(ref.dtype)
            stat[0:1, to] = m_ref[:, cols]
            stat[1:2, to] = total


def join_cores_body(own_ref, recv_ref, own_stat, recv_stat, out_ref):
    m1, l1 = own_stat[0:1, :], own_stat[1:2, :]
    m2, l2 = recv_stat[0:1, :], recv_stat[1:2, :]
    top = jnp.maximum(m1, m2)
    w1 = l1 * jnp.exp2(m1 - top)
    w2 = l2 * jnp.exp2(m2 - top)
    share = 1.0 / (w1 + w2)
    joined = own_ref[...] * (w1 * share) + recv_ref[...].astype(F32) * (w2 * share)
    out_ref[...] = joined.T.astype(BF16).reshape(8, 128, 128)


def merged_weight_body(ids, ow_ref, b00, b01, b10, b11, out_ref):
    l, c = ids[3], ids[4]
    total = None
    for dl, dc, ref in ((0, 0, b00), (0, 1, b01), (1, 0, b10), (1, 1, b11)):
        t = jnp.where(dl == 1, 1 - l, l) * 2 + jnp.where(dc == 1, 1 - c, c)
        part = dot_nn(ow_ref[:, pl.ds(pl.multiple_of(t * 1024, 1024), 1024)], ref[...])
        total = part if total is None else total + part
    out_ref[...] = total.astype(BF16)


def hidden_part_body(ids, hid_ref, cw_ref, own_ref, send_ref, out):
    c = ids[4]
    out[...] = dot_nn(hid_ref[...], cw_ref[...])
    for half in range(2):
        rows = slice(half * 64, half * 64 + 64)
        own_ref[rows, :] = out[pl.ds(pl.multiple_of(half * 128 + c * 64, 64), 64), :]
        send_ref[rows, :] = out[pl.ds(pl.multiple_of(half * 128 + (1 - c) * 64, 64), 64), :].astype(BF16)


def embed_body(codes_ref, table_ref, out_ref):
    vocab = lax.broadcasted_iota(jnp.int32, (64, 1024), 1)
    for n in range(3):
        hit = (vocab == codes_ref[:, n : n + 1]).astype(BF16)
        out_ref[n] = dot_nn(hit, table_ref[n]).astype(BF16)


def relay_body(lo_in, hi_in, w_in, lo_ref, hi_ref, w_ref):
    lo_ref[...] = lo_in[...]
    hi_ref[...] = hi_in[...]
    w_ref[...] = w_in[...]


def pack_body(*refs):
    for n in range(4):
        refs[4][n] = refs[n][...]


def project_body(ids, att_ref, w_ref, wo_ref, h_own_ref, h_recv_ref, own_ref, send_ref, out):
    z, l, c = ids[2], ids[3], ids[4]
    a_own = att_ref[pl.ds(c * 4, 4)]
    a_oth = att_ref[pl.ds((1 - c) * 4, 4)]
    a_own = jnp.concatenate([a_own[i] for i in range(4)], 1)
    a_oth = jnp.concatenate([a_oth[i] for i in range(4)], 1)
    for dz in range(4):
        col = pl.multiple_of(((z + 4 - dz) % 4) * 256, 256)
        out[:, pl.ds(col, 256)] = dot_nn(a_own, w_ref[dz]) + dot_nn(a_oth, wo_ref[dz])
    out[...] += h_own_ref[...] + h_recv_ref[...].astype(F32)
    own_ref[...] = out[pl.ds(pl.multiple_of(l * 64, 64), 64), :]
    send_ref[...] = out[pl.ds(pl.multiple_of((1 - l) * 64, 64), 64), :].astype(BF16)


def rms(stream):
    return lax.rsqrt(jnp.mean(stream * stream, -1, keepdims=True) + 1e-05)


def split_dot(a, b):
    high = a.astype(BF16)
    low = (a - high.astype(F32)).astype(BF16)
    return dot_nn(high, b) + dot_nn(low, b)


def depth_body(
    own_ref, recv_ref, embed_ref, codes_ref, wt_hbm, tab_hbm, loss_ref, dctx_ref, wt, tab, sems,
):
    copies = [pltpu.make_async_copy(wt_hbm.at[i], wt.at[i], sems.at[i]) for i in range(4)]
    copies += [pltpu.make_async_copy(tab_hbm.at[i], tab.at[i], sems.at[4 + i]) for i in range(4)]
    copies[0].start()
    copies[1].start()
    copies[2].start()
    n = 64
    context = own_ref[...] + recv_ref[...].astype(F32)
    stream = jnp.concatenate([context] + [context + embed_ref[i].astype(F32) for i in range(3)], 0)
    r1 = rms(stream)
    normed = (stream * r1).astype(BF16)
    qkv = []
    for i in range(3):
        copies[i].wait()
        copies[3 + i].start()
        qkv.append(dot_nn(normed, wt[i]))
    q, k, v = qkv
    at = lambda a, i: a[i * n : (i + 1) * n]
    pairs = [(i, j) for i in range(4) for j in range(i + 1)]
    lane = lax.broadcasted_iota(jnp.int32, (1024, 128), 0) // 64
    head = lax.broadcasted_iota(jnp.int32, (1024, 128), 1)
    gather_heads = (lane == head).astype(BF16)
    head_t = lax.broadcasted_iota(jnp.int32, (128, 1024), 0)
    lane_t = lax.broadcasted_iota(jnp.int32, (128, 1024), 1) // 64
    spread_heads = (lane_t == head_t).astype(BF16)
    prod = jnp.concatenate([at(q, i) * at(k, j) for i, j in pairs], 0)
    scores = split_dot(prod, gather_heads) * 0.125
    score = {pair: at(scores, number) for number, pair in enumerate(pairs)}
    weight = {}
    for i in range(4):
        top = functools.reduce(jnp.maximum, [score[i, j] for j in range(i + 1)])
        es = [jnp.exp(score[i, j] - top) for j in range(i + 1)]
        total = functools.reduce(jnp.add, es)
        for j in range(i + 1):
            weight[i, j] = es[j] / total
    spread = dot_nn(jnp.concatenate([weight[p] for p in pairs], 0).astype(BF16), spread_heads)
    wide = {pair: at(spread, number) for number, pair in enumerate(pairs)}
    mixed = jnp.concatenate(
        [functools.reduce(jnp.add, [wide[i, j] * at(v, j) for j in range(i + 1)]) for i in range(4)], 0
    ).astype(BF16)
    copies[3].wait()
    copies[6].start()
    update = dot_nn(mixed, wt[3])
    out = stream + update
    r2 = rms(out)
    final = (out * r2).astype(BF16)
    loss = jnp.zeros((n, 1), F32)
    dfinal = []
    scale = 3.0 / 1024**0.5
    vocab = lax.broadcasted_iota(jnp.int32, (n, 1024), 1)
    for i in range(4):
        copies[4 + i].wait()
        if i == 0:
            copies[7].start()
        logits = dot_nt(at(final, i), tab[i]) * scale
        top = jnp.max(logits, -1, keepdims=True)
        e = jnp.exp(logits - top)
        total = jnp.sum(e, -1, keepdims=True)
        hit = vocab == codes_ref[:, i : i + 1]
        picked = jnp.sum(jnp.where(hit, logits, 0.0), -1, keepdims=True)
        loss = loss + top + jnp.log(total) - picked
        dlogits = (e / total - hit.astype(F32)).astype(BF16)
        dfinal.append(dot_nn(dlogits, tab[i]) * scale)
    loss_ref[...] = jnp.broadcast_to(loss, (n, 128))
    dfinal = jnp.concatenate(dfinal, 0)
    dout = r2 * (dfinal - out * (r2 * r2) * jnp.mean(dfinal * out, -1, keepdims=True))
    dmixed = dot_nt(dout.astype(BF16), wt[3])
    dprod = jnp.concatenate([at(dmixed, i) * at(v, j) for i, j in pairs], 0)
    dweights = split_dot(dprod, gather_heads)
    dweight = {pair: at(dweights, number) for number, pair in enumerate(pairs)}
    dscore = []
    for i in range(4):
        mean = functools.reduce(jnp.add, [weight[i, j] * dweight[i, j] for j in range(i + 1)])
        for j in range(i + 1):
            dscore.append(weight[i, j] * (dweight[i, j] - mean) * 0.125)
    spread = dot_nn(jnp.concatenate(dscore, 0).astype(BF16), spread_heads)
    dwide = {pair: at(spread, number) for number, pair in enumerate(pairs)}
    add = lambda terms: functools.reduce(jnp.add, terms)
    dq = jnp.concatenate([add([dwide[i, j] * at(k, j) for j in range(i + 1)]) for i in range(4)], 0)
    dk = jnp.concatenate([add([dwide[i, j] * at(q, i) for i in range(j, 4)]) for j in range(4)], 0)
    dv = jnp.concatenate([add([wide[i, j] * at(dmixed, i) for i in range(j, 4)]) for j in range(4)], 0)
    dnormed = dot_nt(dq.astype(BF16), wt[0]) + dot_nt(dk.astype(BF16), wt[1]) + dot_nt(dv.astype(BF16), wt[2])
    dstream = dout + r1 * (dnormed - stream * (r1 * r1) * jnp.mean(dnormed * stream, -1, keepdims=True))
    dctx_ref[...] = add([at(dstream, i) for i in range(4)]).astype(BF16)


def grad_body(ids, d0, d1, d2, d3, cw_ref, out_ref, rows):
    l, c = ids[3], ids[4]
    for dl, dc, ref in ((0, 0, d0), (0, 1, d1), (1, 0, d2), (1, 1, d3)):
        t = jnp.where(dl == 1, 1 - l, l) * 2 + jnp.where(dc == 1, 1 - c, c)
        rows[pl.ds(pl.multiple_of(t * 64, 64), 64), :] = ref[...]
    out_ref[...] = dot_nt(rows[...], cw_ref[...]).astype(BF16)


def per_device(hidden_in, queries, keys, values, out_weight, context_weight, codes, table, depth_weights):
    coords = [lax.axis_index(name) for name in AXES]
    h, x, z, l, c = coords
    ids = jnp.stack(coords).astype(jnp.int32)

    keep, send, cw_cols = call(
        split_rows_body, (shape(8, 128, 384), shape(4, 128, 384), shape(1024, 256)), [SM] + [ANY] * 4,
        ids, queries, keys, values, context_weight,
        scratch=[pltpu.VMEM((3, 256, 512), BF16), pltpu.SemaphoreType.DMA((4,))], limit=60, nbytes=3 << 20,
    )
    full = lax.dynamic_update_slice(keep, move(send, other_core), ((1 - c) * 4, 0, 0))
    mine = lax.all_to_all(full, ("h", "z"), 0, 0, tiled=True)

    cw_l = move(cw_cols, l_swap)
    cw_c = move(cw_cols, other_core)
    cw_lc = move(cw_l, other_core)
    h_own, h_send = call(
        hidden_part_body, (shape(128, 1024, dtype=F32), shape(128, 1024)), [SM] + [VM] * 2,
        ids, hidden_in, context_weight, scratch=[pltpu.VMEM((256, 1024), F32)], flops=1 << 29, nbytes=3 << 20,
    )
    merged = call(
        merged_weight_body, shape(512, 256), [SM] + [VM] * 5, ids, out_weight, cw_cols, cw_c, cw_l, cw_lc,
        flops=1 << 30, nbytes=6 << 20,
    )
    half = shape(4, 128, 256)
    low, high, q = call(
        take_rows_body, (half, half, shape(8, 128, 128)), [VM], mine, after=(h_own, merged), nbytes=1 << 20
    )
    up_lo, down_hi = move(low, x_up), move(high, x_down)
    q_o = move(q, other_core)
    up_hi, down_lo = move(high, x_up), move(low, x_down)
    stats = (shape(128, 2048, dtype=F32), shape(1, 2048, dtype=F32), shape(1, 2048, dtype=F32))
    carry = call(own_block_body, stats, [SM] + [VM] * 4, ids, q, q_o, low, high, flops=4 << 30, nbytes=2 << 20)
    relay_lo, relay_hi, merged = call(
        relay_body, (half, half, shape(512, 256)), [VM] * 3, up_lo, down_hi, merged, after=carry[1:2], nbytes=1 << 20
    )
    far_lo, far_hi = move(relay_lo, x_up), move(relay_hi, x_down)
    carry = call(
        near_blocks_body, stats, [SM] + [VM] * 9, ids, q, q_o, up_lo, up_hi, down_lo, down_hi, *carry,
        aliases={7: 0, 8: 1, 9: 2}, flops=4 << 30, nbytes=4 << 20,
    )
    pieces = [merged] + [move(merged, z_by(n)) for n in (1, 2, 3)]
    h_recv = move(h_send, other_core)
    own, send, own_stat, send_stat = call(
        far_block_body,
        (shape(128, 1024, dtype=F32), shape(128, 1024), shape(8, 1024, dtype=F32), shape(8, 1024, dtype=F32)),
        [SM] + [VM] * 7, ids, q, q_o, far_lo, far_hi, *carry,
        scratch=[pltpu.VMEM(s.shape, s.dtype) for s in stats], flops=3 << 30, nbytes=3 << 20,
    )
    attended = call(
        join_cores_body, shape(8, 128, 128), [VM] * 4,
        own, move(send, other_core), own_stat, move(send_stat, other_core), nbytes=1 << 20,
    )
    merged = call(pack_body, shape(4, 512, 256), [VM] * 4, *pieces, after=(own_stat,), nbytes=2 << 20)
    merged_o = move(merged, other_core)
    embedded = call(
        embed_body, shape(3, 64, 1024), [VM] * 2, codes, table, after=(own_stat,), flops=3 << 27, nbytes=8 << 20,
    )
    attended = lax.all_to_all(attended, ("h", "z"), 0, 0, tiled=True)

    own, send = call(
        project_body, (shape(64, 1024, dtype=F32), shape(64, 1024)), [SM] + [VM] * 5,
        ids, attended, merged, merged_o, h_own, h_recv, after=(embedded,),
        scratch=[pltpu.VMEM((128, 1024), F32)], flops=1 << 28, nbytes=3 << 20,
    )
    recv = move(send, l_swap)
    losses, dcontext = call(
        depth_body, (shape(64, 128, dtype=F32), shape(64, 1024)), [VM] * 4 + [ANY] * 2,
        own, recv, embedded, codes, depth_weights, table,
        scratch=[pltpu.VMEM((4, 1024, 1024), BF16), pltpu.VMEM((4, 1024, 1024), BF16), pltpu.SemaphoreType.DMA((8,))],
        limit=58, flops=12 << 30, nbytes=17 << 20,
    )
    grad = call(
        grad_body, shape(256, 1024), [SM] + [VM] * 5, ids,
        dcontext, move(dcontext, other_core), move(dcontext, l_swap), move(dcontext, lc_swap), context_weight,
        scratch=[pltpu.VMEM((256, 1024), BF16)], flops=1 << 29, nbytes=3 << 20,
    )
    return losses[:, 0], grad


def solution(mesh):
    fine = Mesh(mesh.devices.reshape(SIZES), AXES)
    seq, tp = AXES[:3], AXES[3:]
    return jax.shard_map(
        per_device,
        mesh=fine,
        in_specs=(
            P(seq, tp), P(seq, tp), P(seq, tp), P(seq, tp), P(tp, None), P(tp, None), P(seq + tp, None), P(), P(),
        ),
        out_specs=(P(seq + tp), P(seq, tp)),
        check_vma=False,
    )
```

```python
import functools
import itertools

import jax
import jax.numpy as jnp
from jax import lax
from jax.experimental import pallas as pl
from jax.experimental.pallas import tpu as pltpu
from jax.sharding import Mesh, PartitionSpec as P

HD = 128
DHEADS = 16
F32 = jnp.float32
BF16 = jnp.bfloat16
AXES = ("h", "x", "z", "l", "c")
SIZES = (2, 4, 4, 2, 2)
LOG2E = 1.4426950408889634
NEG = -1e30
VM = pl.BlockSpec(memory_space=pltpu.VMEM)
ANY = pl.BlockSpec(memory_space=pl.ANY)


def flat(coords):
    number = 0
    for coord, size in zip(coords, SIZES):
        number = number * size + coord
    return number


def move(array, target):
    pairs = []
    for coords in itertools.product(*map(range, SIZES)):
        pairs.append((flat(coords), flat(target(*coords))))
    return lax.ppermute(array, AXES, pairs)


def other_core(h, x, z, l, c):
    return h, x, z, l, 1 - c


def x_up(h, x, z, l, c):
    return h, (x + 1) % 4, z, l, c


def z_by(n):
    return lambda h, x, z, l, c: (h, x, (z + n) % 4, l, c)


def x_down(h, x, z, l, c):
    return h, (x + 3) % 4, z, l, c


def l_swap(h, x, z, l, c):
    return h, x, z, 1 - l, c


def call(body, out_shape, in_specs, *args, after=(), scratch=(), limit=16, flops=0, nbytes=0, aliases=None, out_specs=None):
    if out_specs is None:
        out_specs = jax.tree.map(lambda _: VM, out_shape)
    reads = len(args)

    def run(*refs):
        body(*refs[:reads], *refs[reads + len(after) :])

    args = args + tuple(after)
    in_specs = in_specs + [ANY] * len(after)
    return pl.pallas_call(
        run,
        out_shape=out_shape,
        in_specs=in_specs,
        out_specs=out_specs,
        scratch_shapes=list(scratch),
        input_output_aliases=aliases or {},
        compiler_params=pltpu.CompilerParams(vmem_limit_bytes=limit * 1024 * 1024),
        cost_estimate=pl.CostEstimate(flops=flops, bytes_accessed=nbytes, transcendentals=0),
    )(*args)


def shape(*dims, dtype=BF16):
    return jax.ShapeDtypeStruct(dims, dtype)


def dot_nn(a, b):
    return lax.dot_general(a, b, (((1,), (0,)), ((), ())), preferred_element_type=F32)


def dot_nt(a, b):
    return lax.dot_general(a, b, (((1,), (1,)), ((), ())), preferred_element_type=F32)


def dot_tn(a, b):
    return lax.dot_general(a, b, (((0,), (0,)), ((), ())), preferred_element_type=F32)


def split_rows_body(q_hbm, k_hbm, v_hbm, w_hbm, keep_ref, send_ref, cols_ref, local, sems):
    c = lax.axis_index("c")
    copies = [pltpu.make_async_copy(ref, local.at[n], sems.at[n]) for n, ref in enumerate((q_hbm, k_hbm, v_hbm))]
    cols = pl.ds(pl.multiple_of(lax.axis_index("z") * 256, 256), 256)
    copies.append(pltpu.make_async_copy(w_hbm.at[:, cols], cols_ref, sems.at[3]))
    for copy in copies:
        copy.start()
    for part in range(3):
        copies[part].wait()
        for half in range(2):
            mine = pl.ds(pl.multiple_of(half * 128 + c * 64, 64), 64)
            theirs = pl.ds(pl.multiple_of(half * 128 + (1 - c) * 64, 64), 64)
            for head in range(4):
                cols = slice(head * 128, head * 128 + 128)
                to = slice(part * 128, part * 128 + 128)
                keep_ref[c * 4 + head, half * 64 : half * 64 + 64, to] = local[part, mine, cols]
                send_ref[head, half * 64 : half * 64 + 64, to] = local[part, theirs, cols]
    copies[3].wait()


def attend(state, q, keys, vals, start, mask=None):
    acc_ref, m_ref, l_ref = state
    cols = slice(start, start + 512)
    s = dot_nt(keys, q) * (LOG2E / HD**0.5)
    if mask is not None:
        s = jnp.where(mask, s, NEG)
    old = m_ref[:, cols]
    new = jnp.maximum(old, jnp.max(s, 0, keepdims=True))
    p = jnp.exp2(s - new)
    alpha = jnp.exp2(old - new)
    m_ref[:, cols] = new
    l_ref[:, cols] = l_ref[:, cols] * alpha + jnp.sum(p, 0, keepdims=True)
    acc_ref[:, cols] = acc_ref[:, cols] * alpha + dot_tn(vals, p.astype(BF16))


def rows_of(ref, first, col):
    return ref[first : first + 4, :, col : col + 128].reshape(512, 128)


def take_rows_body(r_ref, lo_ref, hi_ref, q_ref):
    q_ref[...] = r_ref[:, :, 0:128]
    lo_ref[...] = r_ref[0:4, :, 128:384]
    hi_ref[...] = r_ref[4:8, :, 128:384]


def own_block_body(q_ref, q_o_ref, lo_ref, hi_ref, w_in, acc_ref, m_ref, l_ref, w_ref):
    w_ref[...] = w_in[...]
    state = (acc_ref, m_ref, l_ref)
    c = lax.axis_index("c")
    m_ref[...] = jnp.full_like(m_ref, 0.1 * NEG)
    l_ref[...] = jnp.zeros_like(l_ref)
    acc_ref[...] = jnp.zeros_like(acc_ref)
    key_row = lax.broadcasted_iota(jnp.int32, (512, 512), 0)
    q_row = lax.broadcasted_iota(jnp.int32, (512, 512), 1)
    place = lambda row, core: (row // 64) * 128 + core * 64 + row % 64
    key_place = place(key_row, c)
    for section, (ref, core) in enumerate(((q_ref, c), (q_o_ref, 1 - c))):
        mask = key_place <= place(q_row, core)
        for h, kv in enumerate((lo_ref, hi_ref)):
            q = rows_of(ref, h * 4, 0)
            attend(state, q, rows_of(kv, 0, 0), rows_of(kv, 0, 128), h * 1024 + section * 512, mask)
        attend(state, q, rows_of(lo_ref, 0, 0), rows_of(lo_ref, 0, 128), 1024 + section * 512)


def low_step(state, qs, kv, earlier):
    for section, ref in enumerate(qs):
        attend(state, rows_of(ref, 4, 0), rows_of(kv, 0, 0), rows_of(kv, 0, 128), 1024 + section * 512)

    @pl.when(earlier)
    def _():
        for section, ref in enumerate(qs):
            attend(state, rows_of(ref, 0, 0), rows_of(kv, 0, 0), rows_of(kv, 0, 128), section * 512)


def high_step(state, qs, kv, earlier):
    @pl.when(earlier)
    def _():
        for section, ref in enumerate(qs):
            attend(state, rows_of(ref, 4, 0), rows_of(kv, 0, 0), rows_of(kv, 0, 128), 1024 + section * 512)


def carry_over(ins, outs):
    for source, target in zip(ins, outs):
        target[...] = source[...]
    return outs


def first_blocks_body(
    q_ref, q_o_ref, up_lo, down_hi, low, high, acc_in, m_in, l_in, acc_ref, m_ref, l_ref, lo_ref, hi_ref
):
    carry_over((low, high), (lo_ref, hi_ref))
    state = carry_over((acc_in, m_in, l_in), (acc_ref, m_ref, l_ref))
    x = lax.axis_index("x")
    low_step(state, (q_ref, q_o_ref), up_lo, x > 0)
    high_step(state, (q_ref, q_o_ref), down_hi, x == 3)


def far_blocks_body(q_ref, q_o_ref, lo, hi, acc_in, m_in, l_in, acc_ref, m_ref, l_ref):
    state = carry_over((acc_in, m_in, l_in), (acc_ref, m_ref, l_ref))
    earlier = lax.axis_index("x") >= 2
    low_step(state, (q_ref, q_o_ref), lo, earlier)
    high_step(state, (q_ref, q_o_ref), hi, earlier)


def last_blocks_body(
    q_ref, q_o_ref, up_hi, down_lo, acc_in, m_in, l_in, own_ref, send_ref, own_stat, send_stat, acc_ref, m_ref, l_ref
):
    state = carry_over((acc_in, m_in, l_in), (acc_ref, m_ref, l_ref))
    x = lax.axis_index("x")
    high_step(state, (q_ref, q_o_ref), up_hi, x > 0)
    low_step(state, (q_ref, q_o_ref), down_lo, x == 3)
    for section, (ref, stat) in enumerate(((own_ref, own_stat), (send_ref, send_stat))):
        for h in range(2):
            cols = slice(h * 1024 + section * 512, h * 1024 + section * 512 + 512)
            to = slice(h * 512, h * 512 + 512)
            total = l_ref[:, cols]
            ref[:, to] = (acc_ref[:, cols] / jnp.maximum(total, 0.5)).astype(ref.dtype)
            stat[0:1, to] = m_ref[:, cols]
            stat[1:2, to] = total


def join_cores_body(own_ref, recv_ref, own_stat, recv_stat, out_ref):
    m1, l1 = own_stat[0:1, :], own_stat[1:2, :]
    m2, l2 = recv_stat[0:1, :], recv_stat[1:2, :]
    top = jnp.maximum(m1, m2)
    w1 = l1 * jnp.exp2(m1 - top)
    w2 = l2 * jnp.exp2(m2 - top)
    share = 1.0 / (w1 + w2)
    joined = own_ref[...] * (w1 * share) + recv_ref[...].astype(F32) * (w2 * share)
    out_ref[...] = joined.T.astype(BF16).reshape(8, 128, 128)


def merged_weight_body(ow_ref, b00, b01, b10, b11, out_ref):
    l, c = lax.axis_index("l"), lax.axis_index("c")
    total = None
    for dl, dc, ref in ((0, 0, b00), (0, 1, b01), (1, 0, b10), (1, 1, b11)):
        t = jnp.where(dl == 1, 1 - l, l) * 2 + jnp.where(dc == 1, 1 - c, c)
        part = dot_nn(ow_ref[:, pl.ds(pl.multiple_of(t * 1024, 1024), 1024)], ref[...])
        total = part if total is None else total + part
    out_ref[...] = total.astype(BF16)


def hidden_part_body(hid_ref, cw_ref, own_ref, send_ref, out):
    c = lax.axis_index("c")
    out[...] = dot_nn(hid_ref[...], cw_ref[...])
    for half in range(2):
        rows = slice(half * 64, half * 64 + 64)
        own_ref[rows, :] = out[pl.ds(pl.multiple_of(half * 128 + c * 64, 64), 64), :]
        send_ref[rows, :] = out[pl.ds(pl.multiple_of(half * 128 + (1 - c) * 64, 64), 64), :].astype(BF16)


def embed_body(codes_ref, table_ref, out_ref):
    vocab = lax.broadcasted_iota(jnp.int32, (64, 1024), 1)
    for n in range(3):
        hit = (vocab == codes_ref[:, n : n + 1]).astype(BF16)
        out_ref[n] = dot_nn(hit, table_ref[n]).astype(BF16)


def relay_body(lo_in, hi_in, lo_ref, hi_ref):
    carry_over((lo_in, hi_in), (lo_ref, hi_ref))


def pack_body(*refs):
    for n in range(4):
        refs[4][n] = refs[n][...]


def project_body(att_ref, w_ref, wo_ref, h_own_ref, h_recv_ref, own_ref, send_ref, out):
    z, l, c = lax.axis_index("z"), lax.axis_index("l"), lax.axis_index("c")
    a_own = att_ref[pl.ds(c * 4, 4)]
    a_oth = att_ref[pl.ds((1 - c) * 4, 4)]
    a_own = jnp.concatenate([a_own[i] for i in range(4)], 1)
    a_oth = jnp.concatenate([a_oth[i] for i in range(4)], 1)
    for dz in range(4):
        col = pl.multiple_of(((z + 4 - dz) % 4) * 256, 256)
        out[:, pl.ds(col, 256)] = dot_nn(a_own, w_ref[dz]) + dot_nn(a_oth, wo_ref[dz])
    out[...] += h_own_ref[...] + h_recv_ref[...].astype(F32)
    own_ref[...] = out[pl.ds(pl.multiple_of(l * 64, 64), 64), :]
    send_ref[...] = out[pl.ds(pl.multiple_of((1 - l) * 64, 64), 64), :].astype(BF16)


def rms(stream):
    return lax.rsqrt(jnp.mean(stream * stream, -1, keepdims=True) + 1e-05)


def depth_body(
    own_ref, recv_ref, embed_ref, codes_ref, wt_hbm, tab_hbm, loss_ref, dctx_ref, wt, tab, sems,
):
    copies = [pltpu.make_async_copy(wt_hbm.at[i], wt.at[i], sems.at[i]) for i in range(4)]
    copies += [pltpu.make_async_copy(tab_hbm.at[i], tab.at[i], sems.at[4 + i]) for i in range(4)]
    for copy in copies:
        copy.start()
    n = 64
    context = own_ref[...] + recv_ref[...].astype(F32)
    stream = jnp.concatenate([context] + [context + embed_ref[i].astype(F32) for i in range(3)], 0)
    r1 = rms(stream)
    normed = (stream * r1).astype(BF16)
    qkv = []
    for i in range(3):
        copies[i].wait()
        qkv.append(dot_nn(normed, wt[i]))
    q, k, v = qkv
    at = lambda a, i: a[i * n : (i + 1) * n]
    pairs = [(i, j) for i in range(4) for j in range(i + 1)]
    lane = lax.broadcasted_iota(jnp.int32, (1024, 128), 0) // 64
    head = lax.broadcasted_iota(jnp.int32, (1024, 128), 1)
    gather_heads = (lane == head).astype(BF16)
    head_t = lax.broadcasted_iota(jnp.int32, (128, 1024), 0)
    lane_t = lax.broadcasted_iota(jnp.int32, (128, 1024), 1) // 64
    spread_heads = (lane_t == head_t).astype(BF16)
    prod = jnp.concatenate([at(q, i) * at(k, j) for i, j in pairs], 0)
    scores = dot_nn(prod.astype(BF16), gather_heads) * 0.125
    score = {pair: at(scores, number) for number, pair in enumerate(pairs)}
    weight = {}
    for i in range(4):
        top = functools.reduce(jnp.maximum, [score[i, j] for j in range(i + 1)])
        es = [jnp.exp(score[i, j] - top) for j in range(i + 1)]
        total = functools.reduce(jnp.add, es)
        for j in range(i + 1):
            weight[i, j] = es[j] / total
    spread = dot_nn(jnp.concatenate([weight[p] for p in pairs], 0).astype(BF16), spread_heads)
    wide = {pair: at(spread, number) for number, pair in enumerate(pairs)}
    mixed = jnp.concatenate(
        [functools.reduce(jnp.add, [wide[i, j] * at(v, j) for j in range(i + 1)]) for i in range(4)], 0
    ).astype(BF16)
    copies[3].wait()
    update = dot_nn(mixed, wt[3])
    out = stream + update
    r2 = rms(out)
    final = (out * r2).astype(BF16)
    loss = jnp.zeros((n, 1), F32)
    dfinal = []
    scale = 3.0 / 1024**0.5
    vocab = lax.broadcasted_iota(jnp.int32, (n, 1024), 1)
    for i in range(4):
        copies[4 + i].wait()
        logits = dot_nt(at(final, i), tab[i]) * scale
        top = jnp.max(logits, -1, keepdims=True)
        e = jnp.exp(logits - top)
        total = jnp.sum(e, -1, keepdims=True)
        hit = vocab == codes_ref[:, i : i + 1]
        picked = jnp.sum(jnp.where(hit, logits, 0.0), -1, keepdims=True)
        loss = loss + top + jnp.log(total) - picked
        dlogits = (e / total - hit.astype(F32)).astype(BF16)
        dfinal.append(dot_nn(dlogits, tab[i]) * scale)
    loss_ref[...] = jnp.broadcast_to(loss, (n, 128)).T[0:1, :]
    dfinal = jnp.concatenate(dfinal, 0)
    dout = r2 * (dfinal - out * (r2 * r2) * jnp.mean(dfinal * out, -1, keepdims=True))
    dmixed = dot_nt(dout.astype(BF16), wt[3])
    dprod = jnp.concatenate([at(dmixed, i) * at(v, j) for i, j in pairs], 0)
    dweights = dot_nn(dprod.astype(BF16), gather_heads)
    dweight = {pair: at(dweights, number) for number, pair in enumerate(pairs)}
    dscore = []
    for i in range(4):
        mean = functools.reduce(jnp.add, [weight[i, j] * dweight[i, j] for j in range(i + 1)])
        for j in range(i + 1):
            dscore.append(weight[i, j] * (dweight[i, j] - mean) * 0.125)
    spread = dot_nn(jnp.concatenate(dscore, 0).astype(BF16), spread_heads)
    dwide = {pair: at(spread, number) for number, pair in enumerate(pairs)}
    add = lambda terms: functools.reduce(jnp.add, terms)
    dq = jnp.concatenate([add([dwide[i, j] * at(k, j) for j in range(i + 1)]) for i in range(4)], 0)
    dk = jnp.concatenate([add([dwide[i, j] * at(q, i) for i in range(j, 4)]) for j in range(4)], 0)
    dv = jnp.concatenate([add([wide[i, j] * at(dmixed, i) for i in range(j, 4)]) for j in range(4)], 0)
    dnormed = dot_nt(dq.astype(BF16), wt[0]) + dot_nt(dk.astype(BF16), wt[1]) + dot_nt(dv.astype(BF16), wt[2])
    dstream = dout + r1 * (dnormed - stream * (r1 * r1) * jnp.mean(dnormed * stream, -1, keepdims=True))
    dctx_ref[...] = add([at(dstream, i) for i in range(4)]).astype(BF16)


def grad_chip_body(own_ref, other_ref, cw_ref, out_ref, rows):
    c = lax.axis_index("c")
    rows[pl.ds(pl.multiple_of(c * 64, 64), 64), :] = own_ref[...]
    rows[pl.ds(pl.multiple_of((1 - c) * 64, 64), 64), :] = other_ref[...]
    out_ref[...] = dot_nt(rows[...], cw_ref[...]).astype(BF16)


def grad_body(chip_ref, l_ref, lc_ref, cw_ref, out_ref, rows):
    l, c = lax.axis_index("l"), lax.axis_index("c")
    rows[pl.ds(pl.multiple_of(c * 64, 64), 64), :] = l_ref[...]
    rows[pl.ds(pl.multiple_of((1 - c) * 64, 64), 64), :] = lc_ref[...]
    out_ref[pl.ds(pl.multiple_of(l * 128, 128), 128), :] = chip_ref[...]
    out_ref[pl.ds(pl.multiple_of((1 - l) * 128, 128), 128), :] = dot_nt(rows[...], cw_ref[...]).astype(BF16)


def per_device(hidden_in, queries, keys, values, out_weight, context_weight, codes, table, depth_weights):
    c = lax.axis_index("c")

    keep, send, cw_cols = call(
        split_rows_body, (shape(8, 128, 384), shape(4, 128, 384), shape(1024, 256)), [ANY] * 4,
        queries, keys, values, context_weight,
        scratch=[pltpu.VMEM((3, 256, 512), BF16), pltpu.SemaphoreType.DMA((4,))], limit=60, nbytes=3 << 20,
    )
    full = lax.dynamic_update_slice(keep, move(send, other_core), ((1 - c) * 4, 0, 0))
    mine = lax.all_to_all(full, ("h", "z"), 0, 0, tiled=True)

    cw_l = move(cw_cols, l_swap)
    cw_c = move(cw_cols, other_core)
    cw_lc = move(cw_l, other_core)
    h_own, h_send = call(
        hidden_part_body, (shape(128, 1024, dtype=F32), shape(128, 1024)), [VM] * 2,
        hidden_in, context_weight, scratch=[pltpu.VMEM((256, 1024), F32)], flops=1 << 29, nbytes=3 << 20,
    )
    merged = call(
        merged_weight_body, shape(512, 256), [VM] * 5, out_weight, cw_cols, cw_c, cw_l, cw_lc,
        flops=1 << 30, nbytes=6 << 20,
    )
    half = shape(4, 128, 256)
    low, high, q = call(
        take_rows_body, (half, half, shape(8, 128, 128)), [VM], mine, after=(h_own, merged), nbytes=1 << 20
    )
    up_lo, down_hi = move(low, x_up), move(high, x_down)
    q_o = move(q, other_core)
    stats = (shape(128, 2048, dtype=F32), shape(1, 2048, dtype=F32), shape(1, 2048, dtype=F32))
    *carry, merged = call(
        own_block_body, stats + (shape(512, 256),), [VM] * 5, q, q_o, low, high, merged, flops=4 << 30, nbytes=2 << 20
    )
    pieces = [merged] + [move(merged, z_by(n)) for n in (1, 2, 3)]
    relay_lo, relay_hi = call(relay_body, (half, half), [VM] * 2, up_lo, down_hi, after=carry[1:2], nbytes=1 << 20)
    far_lo, far_hi = move(relay_lo, x_up), move(relay_hi, x_down)
    *carry, low, high = call(
        first_blocks_body, stats + (half, half), [VM] * 9, q, q_o, up_lo, down_hi, low, high, *carry, after=(relay_lo,),
        aliases={6: 0, 7: 1, 8: 2}, flops=3 << 30, nbytes=4 << 20,
    )
    up_hi, down_lo = move(high, x_up), move(low, x_down)
    carry = call(
        far_blocks_body, stats, [VM] * 7, q, q_o, far_lo, far_hi, *carry,
        aliases={4: 0, 5: 1, 6: 2}, flops=3 << 30, nbytes=3 << 20,
    )
    h_recv = move(h_send, other_core)
    embedded = call(embed_body, shape(3, 64, 1024), [VM] * 2, codes, table, after=carry[1:2], flops=3 << 27, nbytes=8 << 20)
    own, send, own_stat, send_stat = call(
        last_blocks_body,
        (shape(128, 1024, dtype=F32), shape(128, 1024), shape(8, 1024, dtype=F32), shape(8, 1024, dtype=F32)),
        [VM] * 7, q, q_o, up_hi, down_lo, *carry, after=(embedded, h_recv, *pieces[1:]),
        scratch=[pltpu.VMEM(s.shape, s.dtype) for s in stats], flops=3 << 30, nbytes=3 << 20,
    )
    attended = call(
        join_cores_body, shape(8, 128, 128), [VM] * 4,
        own, move(send, other_core), own_stat, move(send_stat, other_core), nbytes=1 << 20,
    )
    merged = call(pack_body, shape(4, 512, 256), [VM] * 4, *pieces, after=(own_stat,), nbytes=2 << 20)
    merged_o = move(merged, other_core)
    attended = lax.all_to_all(attended, ("h", "z"), 0, 0, tiled=True)

    own, send = call(
        project_body, (shape(64, 1024, dtype=F32), shape(64, 1024)), [VM] * 5,
        attended, merged, merged_o, h_own, h_recv,
        scratch=[pltpu.VMEM((128, 1024), F32)], flops=1 << 28, nbytes=3 << 20,
    )
    recv = move(send, l_swap)
    losses, dcontext = call(
        depth_body, (shape(1, 64, dtype=F32), shape(64, 1024)), [VM] * 4 + [ANY] * 2,
        own, recv, embedded, codes, depth_weights, table,
        scratch=[pltpu.VMEM((4, 1024, 1024), BF16), pltpu.VMEM((4, 1024, 1024), BF16), pltpu.SemaphoreType.DMA((8,))],
        limit=60, flops=12 << 30, nbytes=17 << 20,
    )
    d_l = move(dcontext, l_swap)
    rows = [pltpu.VMEM((128, 1024), BF16)]
    grad_chip = call(
        grad_chip_body, shape(128, 1024), [VM] * 3, dcontext, move(dcontext, other_core), context_weight,
        scratch=rows, flops=1 << 28, nbytes=3 << 20,
    )
    grad = call(
        grad_body, shape(256, 1024), [VM] * 4, grad_chip, d_l, move(d_l, other_core), context_weight,
        scratch=rows, flops=1 << 28, nbytes=3 << 20,
    )
    return losses.reshape(64), grad


def solution(mesh):
    fine = Mesh(mesh.devices.reshape(SIZES), AXES)
    seq, tp = AXES[:3], AXES[3:]
    return jax.shard_map(
        per_device,
        mesh=fine,
        in_specs=(
            P(seq, tp), P(seq, tp), P(seq, tp), P(seq, tp), P(tp, None), P(tp, None), P(seq + tp, None), P(), P(),
        ),
        out_specs=(P(seq + tp), P(seq, tp)),
        check_vma=False,
    )
```

```python
import functools
import itertools

import jax
import jax.numpy as jnp
from jax import lax
from jax.experimental import pallas as pl
from jax.experimental.pallas import tpu as pltpu
from jax.sharding import Mesh, PartitionSpec as P

HD = 128
DHEADS = 16
F32 = jnp.float32
BF16 = jnp.bfloat16
AXES = ("h", "x", "z", "l", "c")
SIZES = (2, 4, 4, 2, 2)
LOG2E = 1.4426950408889634
NEG = -1e30
VM = pl.BlockSpec(memory_space=pltpu.VMEM)
ANY = pl.BlockSpec(memory_space=pl.ANY)


def flat(coords):
    number = 0
    for coord, size in zip(coords, SIZES):
        number = number * size + coord
    return number


def move(array, target):
    pairs = []
    for coords in itertools.product(*map(range, SIZES)):
        pairs.append((flat(coords), flat(target(*coords))))
    return lax.ppermute(array, AXES, pairs)


def other_core(h, x, z, l, c):
    return h, x, z, l, 1 - c


def x_up(h, x, z, l, c):
    return h, (x + 1) % 4, z, l, c


def z_by(n):
    return lambda h, x, z, l, c: (h, x, (z + n) % 4, l, c)


def x_down(h, x, z, l, c):
    return h, (x + 3) % 4, z, l, c


def l_swap(h, x, z, l, c):
    return h, x, z, 1 - l, c


def call(body, out_shape, in_specs, *args, after=(), scratch=(), limit=16, flops=0, nbytes=0, aliases=None, out_specs=None):
    if out_specs is None:
        out_specs = jax.tree.map(lambda _: VM, out_shape)
    reads = len(args)

    def run(*refs):
        body(*refs[:reads], *refs[reads + len(after) :])

    args = args + tuple(after)
    in_specs = in_specs + [ANY] * len(after)
    return pl.pallas_call(
        run,
        out_shape=out_shape,
        in_specs=in_specs,
        out_specs=out_specs,
        scratch_shapes=list(scratch),
        input_output_aliases=aliases or {},
        compiler_params=pltpu.CompilerParams(vmem_limit_bytes=limit * 1024 * 1024),
        cost_estimate=pl.CostEstimate(flops=flops, bytes_accessed=nbytes, transcendentals=0),
    )(*args)


def shape(*dims, dtype=BF16):
    return jax.ShapeDtypeStruct(dims, dtype)


def dot_nn(a, b):
    return lax.dot_general(a, b, (((1,), (0,)), ((), ())), preferred_element_type=F32)


def dot_nt(a, b):
    return lax.dot_general(a, b, (((1,), (1,)), ((), ())), preferred_element_type=F32)


def dot_tn(a, b):
    return lax.dot_general(a, b, (((0,), (0,)), ((), ())), preferred_element_type=F32)


def split_rows_body(q_hbm, k_hbm, v_hbm, w_hbm, keep_ref, send_ref, cols_ref, local, sems):
    c = lax.axis_index("c")
    copies = [pltpu.make_async_copy(ref, local.at[n], sems.at[n]) for n, ref in enumerate((q_hbm, k_hbm, v_hbm))]
    cols = pl.ds(pl.multiple_of(lax.axis_index("z") * 256, 256), 256)
    copies.append(pltpu.make_async_copy(w_hbm.at[:, cols], cols_ref, sems.at[3]))
    for copy in copies:
        copy.start()
    for part in range(3):
        copies[part].wait()
        for half in range(2):
            mine = pl.ds(pl.multiple_of(half * 128 + c * 64, 64), 64)
            theirs = pl.ds(pl.multiple_of(half * 128 + (1 - c) * 64, 64), 64)
            for head in range(4):
                cols = slice(head * 128, head * 128 + 128)
                to = slice(part * 128, part * 128 + 128)
                keep_ref[c * 4 + head, half * 64 : half * 64 + 64, to] = local[part, mine, cols]
                send_ref[head, half * 64 : half * 64 + 64, to] = local[part, theirs, cols]
    copies[3].wait()


def attend(state, q, keys, vals_t, start, mask=None):
    acc_ref, m_ref, l_ref = state
    for first in range(0, 512, 128):
        cols = slice(start + first, start + first + 128)
        s = dot_nt(keys, q[first : first + 128]) * (LOG2E / HD**0.5)
        if mask is not None:
            s = jnp.where(mask[:, first : first + 128], s, NEG)
        old = m_ref[:, cols]
        new = jnp.maximum(old, jnp.max(s, 0, keepdims=True))
        p = jnp.exp2(s - new)
        alpha = jnp.exp2(old - new)
        m_ref[:, cols] = new
        l_ref[:, cols] = l_ref[:, cols] * alpha + jnp.sum(p, 0, keepdims=True)
        acc_ref[:, cols] = acc_ref[:, cols] * alpha + dot_nn(vals_t, p.astype(BF16))


def rows_of(ref, first):
    return ref[first : first + 4, :, 0:128].reshape(512, 128)


def values_of(ref, first):
    return jnp.concatenate([ref[first + n, :, 128:256] for n in range(4)], 1)


def take_rows_body(r_ref, lo_ref, hi_ref, q_ref):
    q_ref[...] = r_ref[:, :, 0:128]
    for n in range(8):
        ref = lo_ref if n < 4 else hi_ref
        ref[n % 4, :, 0:128] = r_ref[n, :, 128:256]
        ref[n % 4, :, 128:256] = r_ref[n, :, 256:384].T


def carry_over(ins, outs):
    for source, target in zip(ins, outs):
        target[...] = source[...]
    return outs


def own_block_body(q_ref, q_o_ref, lo_in, hi_in, w_in, acc_ref, m_ref, l_ref, w_ref):
    w_ref[...] = w_in[...]
    state = (acc_ref, m_ref, l_ref)
    c = lax.axis_index("c")
    m_ref[...] = jnp.full_like(m_ref, 0.1 * NEG)
    l_ref[...] = jnp.zeros_like(l_ref)
    acc_ref[...] = jnp.zeros_like(acc_ref)
    key_row = lax.broadcasted_iota(jnp.int32, (512, 512), 0)
    q_row = lax.broadcasted_iota(jnp.int32, (512, 512), 1)
    place = lambda row, core: (row // 64) * 128 + core * 64 + row % 64
    key_place = place(key_row, c)
    for section, (ref, core) in enumerate(((q_ref, c), (q_o_ref, 1 - c))):
        mask = key_place <= place(q_row, core)
        for h, kv in enumerate((lo_in, hi_in)):
            attend(state, rows_of(ref, h * 4), rows_of(kv, 0), values_of(kv, 0), h * 1024 + section * 512, mask)
        attend(state, rows_of(ref, 4), rows_of(lo_in, 0), values_of(lo_in, 0), 1024 + section * 512)


def low_step(state, qs, kv, earlier):
    for section, ref in enumerate(qs):
        attend(state, rows_of(ref, 4), rows_of(kv, 0), values_of(kv, 0), 1024 + section * 512)

    @pl.when(earlier)
    def _():
        for section, ref in enumerate(qs):
            attend(state, rows_of(ref, 0), rows_of(kv, 0), values_of(kv, 0), section * 512)


def high_step(state, qs, kv, earlier):
    @pl.when(earlier)
    def _():
        for section, ref in enumerate(qs):
            attend(state, rows_of(ref, 4), rows_of(kv, 0), values_of(kv, 0), 1024 + section * 512)


def first_blocks_body(
    q_ref, q_o_ref, up_lo, down_hi, low, high, acc_in, m_in, l_in, acc_ref, m_ref, l_ref, lo_ref, hi_ref
):
    carry_over((low, high), (lo_ref, hi_ref))
    state = carry_over((acc_in, m_in, l_in), (acc_ref, m_ref, l_ref))
    x = lax.axis_index("x")
    low_step(state, (q_ref, q_o_ref), up_lo, x > 0)
    high_step(state, (q_ref, q_o_ref), down_hi, x == 3)


def far_blocks_body(q_ref, q_o_ref, lo, hi, acc_in, m_in, l_in, acc_ref, m_ref, l_ref):
    state = carry_over((acc_in, m_in, l_in), (acc_ref, m_ref, l_ref))
    earlier = lax.axis_index("x") >= 2
    low_step(state, (q_ref, q_o_ref), lo, earlier)
    high_step(state, (q_ref, q_o_ref), hi, earlier)


def last_blocks_body(
    q_ref, q_o_ref, up_hi, down_lo, acc_in, m_in, l_in, own_ref, send_ref, own_stat, acc_ref, m_ref, l_ref
):
    state = carry_over((acc_in, m_in, l_in), (acc_ref, m_ref, l_ref))
    x = lax.axis_index("x")
    high_step(state, (q_ref, q_o_ref), up_hi, x > 0)
    low_step(state, (q_ref, q_o_ref), down_lo, x == 3)
    send_ref[...] = jnp.zeros_like(send_ref)
    for section in range(2):
        for h in range(2):
            cols = slice(h * 1024 + section * 512, h * 1024 + section * 512 + 512)
            to = slice(h * 512, h * 512 + 512)
            top = m_ref[:, cols]
            total = l_ref[:, cols]
            part = acc_ref[:, cols] / jnp.maximum(total, 0.5)
            if section == 0:
                own_ref[:, to] = part
                own_stat[0:1, to] = top
                own_stat[1:2, to] = total
            else:
                send_ref[0:128, to] = part.astype(BF16)
                for n, value in enumerate((top, total)):
                    for term in range(3):
                        piece = value.astype(BF16)
                        send_ref[128 + n * 16 + term : 129 + n * 16 + term, to] = piece
                        value = value - piece.astype(F32)


def join_cores_body(own_ref, recv_ref, own_stat, out_ref):
    m1, l1 = own_stat[0:1, :], own_stat[1:2, :]
    stat = recv_ref[128:160, :].astype(F32)
    m2 = stat[0:1] + stat[1:2] + stat[2:3]
    l2 = stat[16:17] + stat[17:18] + stat[18:19]
    top = jnp.maximum(m1, m2)
    w1 = l1 * jnp.exp2(m1 - top)
    w2 = l2 * jnp.exp2(m2 - top)
    share = 1.0 / (w1 + w2)
    joined = own_ref[...] * (w1 * share) + recv_ref[0:128, :].astype(F32) * (w2 * share)
    out_ref[...] = joined.T.astype(BF16).reshape(8, 128, 128)


def merged_weight_body(ow_ref, b00, b01, b10, b11, out_ref):
    l, c = lax.axis_index("l"), lax.axis_index("c")
    total = None
    for dl, dc, ref in ((0, 0, b00), (0, 1, b01), (1, 0, b10), (1, 1, b11)):
        t = jnp.where(dl == 1, 1 - l, l) * 2 + jnp.where(dc == 1, 1 - c, c)
        part = dot_nn(ow_ref[:, pl.ds(pl.multiple_of(t * 1024, 1024), 1024)], ref[...])
        total = part if total is None else total + part
    out_ref[...] = total.astype(BF16)


def hidden_part_body(hid_ref, cw_ref, own_ref, send_ref, out):
    c = lax.axis_index("c")
    out[...] = dot_nn(hid_ref[...], cw_ref[...])
    for half in range(2):
        rows = slice(half * 64, half * 64 + 64)
        own_ref[rows, :] = out[pl.ds(pl.multiple_of(half * 128 + c * 64, 64), 64), :]
        send_ref[rows, :] = out[pl.ds(pl.multiple_of(half * 128 + (1 - c) * 64, 64), 64), :].astype(BF16)


def embed_body(codes_ref, table_ref, out_ref):
    vocab = lax.broadcasted_iota(jnp.int32, (64, 1024), 1)
    for n in range(3):
        hit = (vocab == codes_ref[:, n : n + 1]).astype(BF16)
        out_ref[n] = dot_nn(hit, table_ref[n]).astype(BF16)


def relay_body(lo_in, hi_in, lo_ref, hi_ref):
    carry_over((lo_in, hi_in), (lo_ref, hi_ref))


def pack_body(*refs):
    for n in range(4):
        refs[4][n] = refs[n][...]


def project_body(att_ref, w_ref, wo_ref, h_own_ref, h_recv_ref, own_ref, send_ref, out):
    z, l, c = lax.axis_index("z"), lax.axis_index("l"), lax.axis_index("c")
    a_own = att_ref[pl.ds(c * 4, 4)]
    a_oth = att_ref[pl.ds((1 - c) * 4, 4)]
    a_own = jnp.concatenate([a_own[i] for i in range(4)], 1)
    a_oth = jnp.concatenate([a_oth[i] for i in range(4)], 1)
    for dz in range(4):
        col = pl.multiple_of(((z + 4 - dz) % 4) * 256, 256)
        out[:, pl.ds(col, 256)] = dot_nn(a_own, w_ref[dz]) + dot_nn(a_oth, wo_ref[dz])
    out[...] += h_own_ref[...] + h_recv_ref[...].astype(F32)
    own_ref[...] = out[pl.ds(pl.multiple_of(l * 64, 64), 64), :]
    send_ref[...] = out[pl.ds(pl.multiple_of((1 - l) * 64, 64), 64), :].astype(BF16)


def rms(stream):
    return lax.rsqrt(jnp.mean(stream * stream, -1, keepdims=True) + 1e-05)


def depth_body(
    own_ref, recv_ref, embed_ref, codes_ref, wt_hbm, tab_hbm, loss_ref, dctx_ref, wt, tab, sems,
):
    copies = [pltpu.make_async_copy(wt_hbm.at[i], wt.at[i], sems.at[i]) for i in range(4)]
    copies += [pltpu.make_async_copy(tab_hbm.at[i], tab.at[i], sems.at[4 + i]) for i in range(4)]
    for copy in copies:
        copy.start()
    n = 64
    context = own_ref[...] + recv_ref[...].astype(F32)
    stream = jnp.concatenate([context] + [context + embed_ref[i].astype(F32) for i in range(3)], 0)
    r1 = rms(stream)
    normed = (stream * r1).astype(BF16)
    qkv = []
    for i in range(3):
        copies[i].wait()
        qkv.append(dot_nn(normed, wt[i]))
    q, k, v = qkv
    at = lambda a, i: a[i * n : (i + 1) * n]
    pairs = [(i, j) for i in range(1, 4) for j in range(i + 1)]
    lane = lax.broadcasted_iota(jnp.int32, (1024, 128), 0) // 64
    head = lax.broadcasted_iota(jnp.int32, (1024, 128), 1)
    gather_heads = (lane == head).astype(BF16)
    head_t = lax.broadcasted_iota(jnp.int32, (128, 1024), 0)
    lane_t = lax.broadcasted_iota(jnp.int32, (128, 1024), 1) // 64
    spread_heads = (lane_t == head_t).astype(BF16)
    prod = jnp.concatenate([at(q, i) * at(k, j) for i, j in pairs], 0)
    scores = dot_nn(prod.astype(BF16), gather_heads) * 0.125
    score = {pair: at(scores, number) for number, pair in enumerate(pairs)}
    weight = {}
    for i in range(1, 4):
        top = functools.reduce(jnp.maximum, [score[i, j] for j in range(i + 1)])
        es = [jnp.exp(score[i, j] - top) for j in range(i + 1)]
        total = functools.reduce(jnp.add, es)
        for j in range(i + 1):
            weight[i, j] = es[j] / total
    spread = dot_nn(jnp.concatenate([weight[p] for p in pairs], 0).astype(BF16), spread_heads)
    wide = {pair: at(spread, number) for number, pair in enumerate(pairs)}
    mixed = jnp.concatenate(
        [at(v, 0)] + [functools.reduce(jnp.add, [wide[i, j] * at(v, j) for j in range(i + 1)]) for i in range(1, 4)], 0
    ).astype(BF16)
    copies[3].wait()
    update = dot_nn(mixed, wt[3])
    out = stream + update
    r2 = rms(out)
    final = (out * r2).astype(BF16)
    loss = jnp.zeros((n, 1), F32)
    dfinal = []
    scale = 3.0 / 1024**0.5
    vocab = lax.broadcasted_iota(jnp.int32, (n, 1024), 1)
    for i in range(4):
        copies[4 + i].wait()
        logits = dot_nt(at(final, i), tab[i]) * scale
        top = jnp.max(logits, -1, keepdims=True)
        e = jnp.exp(logits - top)
        total = jnp.sum(e, -1, keepdims=True)
        hit = vocab == codes_ref[:, i : i + 1]
        picked = jnp.sum(jnp.where(hit, logits, 0.0), -1, keepdims=True)
        loss = loss + top + jnp.log(total) - picked
        dlogits = (e * (1.0 / total) - hit.astype(F32)).astype(BF16)
        dfinal.append(dot_nn(dlogits, tab[i]) * scale)
    loss_ref[...] = jnp.broadcast_to(loss, (n, 128)).T[0:1, :]
    dfinal = jnp.concatenate(dfinal, 0)
    dout = r2 * (dfinal - out * (r2 * r2) * jnp.mean(dfinal * out, -1, keepdims=True))
    dmixed = dot_nt(dout.astype(BF16), wt[3])
    dprod = jnp.concatenate([at(dmixed, i) * at(v, j) for i, j in pairs], 0)
    dweights = dot_nn(dprod.astype(BF16), gather_heads)
    dweight = {pair: at(dweights, number) for number, pair in enumerate(pairs)}
    dscore = []
    for i in range(1, 4):
        mean = functools.reduce(jnp.add, [weight[i, j] * dweight[i, j] for j in range(i + 1)])
        for j in range(i + 1):
            dscore.append(weight[i, j] * (dweight[i, j] - mean) * 0.125)
    spread = dot_nn(jnp.concatenate(dscore, 0).astype(BF16), spread_heads)
    dwide = {pair: at(spread, number) for number, pair in enumerate(pairs)}
    add = lambda terms: functools.reduce(jnp.add, terms)
    dq = [add([dwide[i, j] * at(k, j) for j in range(i + 1)]) for i in range(1, 4)]
    dq = jnp.concatenate([jnp.zeros((n, 1024), F32)] + dq, 0)
    dk = jnp.concatenate([add([dwide[i, j] * at(q, i) for i in range(max(j, 1), 4)]) for j in range(4)], 0)
    dv = [add([wide[i, j] * at(dmixed, i) for i in range(max(j, 1), 4)]) for j in range(4)]
    dv = jnp.concatenate([dv[0] + at(dmixed, 0)] + dv[1:], 0)
    dnormed = dot_nt(dq.astype(BF16), wt[0]) + dot_nt(dk.astype(BF16), wt[1]) + dot_nt(dv.astype(BF16), wt[2])
    dstream = dout + r1 * (dnormed - stream * (r1 * r1) * jnp.mean(dnormed * stream, -1, keepdims=True))
    dctx_ref[...] = add([at(dstream, i) for i in range(4)]).astype(BF16)


def grad_chip_body(own_ref, other_ref, cw_ref, out_ref, rows):
    c = lax.axis_index("c")
    rows[pl.ds(pl.multiple_of(c * 64, 64), 64), :] = own_ref[...]
    rows[pl.ds(pl.multiple_of((1 - c) * 64, 64), 64), :] = other_ref[...]
    out_ref[...] = dot_nt(rows[...], cw_ref[...]).astype(BF16)


def grad_body(chip_ref, l_ref, lc_ref, cw_ref, out_ref, rows):
    l, c = lax.axis_index("l"), lax.axis_index("c")
    rows[pl.ds(pl.multiple_of(c * 64, 64), 64), :] = l_ref[...]
    rows[pl.ds(pl.multiple_of((1 - c) * 64, 64), 64), :] = lc_ref[...]
    out_ref[pl.ds(pl.multiple_of(l * 128, 128), 128), :] = chip_ref[...]
    out_ref[pl.ds(pl.multiple_of((1 - l) * 128, 128), 128), :] = dot_nt(rows[...], cw_ref[...]).astype(BF16)


def per_device(hidden_in, queries, keys, values, out_weight, context_weight, codes, table, depth_weights):
    c = lax.axis_index("c")

    keep, send, cw_cols = call(
        split_rows_body, (shape(8, 128, 384), shape(4, 128, 384), shape(1024, 256)), [ANY] * 4,
        queries, keys, values, context_weight,
        scratch=[pltpu.VMEM((3, 256, 512), BF16), pltpu.SemaphoreType.DMA((4,))], limit=60, nbytes=3 << 20,
    )
    full = lax.dynamic_update_slice(keep, move(send, other_core), ((1 - c) * 4, 0, 0))
    mine = lax.all_to_all(full, ("h", "z"), 0, 0, tiled=True)

    cw_l = move(cw_cols, l_swap)
    cw_c = move(cw_cols, other_core)
    cw_lc = move(cw_l, other_core)
    h_own, h_send = call(
        hidden_part_body, (shape(128, 1024, dtype=F32), shape(128, 1024)), [VM] * 2,
        hidden_in, context_weight, scratch=[pltpu.VMEM((256, 1024), F32)], flops=1 << 29, nbytes=3 << 20,
    )
    merged = call(
        merged_weight_body, shape(512, 256), [VM] * 5, out_weight, cw_cols, cw_c, cw_l, cw_lc,
        flops=1 << 30, nbytes=6 << 20,
    )
    half = shape(4, 128, 256)
    low, high, q = call(
        take_rows_body, (half, half, shape(8, 128, 128)), [VM], mine, after=(h_own, merged), nbytes=1 << 20
    )
    up_lo, down_hi = move(low, x_up), move(high, x_down)
    q_o = move(q, other_core)
    stats = (shape(128, 2048, dtype=F32), shape(1, 2048, dtype=F32), shape(1, 2048, dtype=F32))
    *carry, merged = call(
        own_block_body, stats + (shape(512, 256),), [VM] * 5, q, q_o, low, high, merged, flops=4 << 30, nbytes=2 << 20
    )
    pieces = [merged] + [move(merged, z_by(n)) for n in (1, 2, 3)]
    relay_lo, relay_hi = call(relay_body, (half, half), [VM] * 2, up_lo, down_hi, after=carry[1:2], nbytes=1 << 20)
    far_lo, far_hi = move(relay_lo, x_up), move(relay_hi, x_down)
    *carry, low, high = call(
        first_blocks_body, stats + (half, half), [VM] * 9, q, q_o, up_lo, down_hi, low, high, *carry, after=(relay_lo,),
        aliases={6: 0, 7: 1, 8: 2}, flops=3 << 30, nbytes=4 << 20,
    )
    up_hi, down_lo = move(high, x_up), move(low, x_down)
    carry = call(
        far_blocks_body, stats, [VM] * 7, q, q_o, far_lo, far_hi, *carry,
        aliases={4: 0, 5: 1, 6: 2}, flops=3 << 30, nbytes=3 << 20,
    )
    h_recv = move(h_send, other_core)
    embedded = call(embed_body, shape(3, 64, 1024), [VM] * 2, codes, table, after=carry[1:2], flops=3 << 27, nbytes=8 << 20)
    own, send, own_stat = call(
        last_blocks_body, (shape(128, 1024, dtype=F32), shape(160, 1024), shape(8, 1024, dtype=F32)),
        [VM] * 7, q, q_o, up_hi, down_lo, *carry, after=(embedded, h_recv, *pieces[1:]),
        scratch=[pltpu.VMEM(s.shape, s.dtype) for s in stats], flops=3 << 30, nbytes=3 << 20,
    )
    joined = move(send, other_core)
    attended = call(join_cores_body, shape(8, 128, 128), [VM] * 3, own, joined, own_stat, nbytes=1 << 20)
    merged = call(pack_body, shape(4, 512, 256), [VM] * 4, *pieces, after=(joined,), nbytes=2 << 20)
    merged_o = move(merged, other_core)
    attended = lax.all_to_all(attended, ("h", "z"), 0, 0, tiled=True)

    own, send = call(
        project_body, (shape(64, 1024, dtype=F32), shape(64, 1024)), [VM] * 5,
        attended, merged, merged_o, h_own, h_recv,
        scratch=[pltpu.VMEM((128, 1024), F32)], flops=1 << 28, nbytes=3 << 20,
    )
    recv = move(send, l_swap)
    losses, dcontext = call(
        depth_body, (shape(1, 64, dtype=F32), shape(64, 1024)), [VM] * 4 + [ANY] * 2,
        own, recv, embedded, codes, depth_weights, table,
        scratch=[pltpu.VMEM((4, 1024, 1024), BF16), pltpu.VMEM((4, 1024, 1024), BF16), pltpu.SemaphoreType.DMA((8,))],
        limit=60, flops=12 << 30, nbytes=17 << 20,
    )
    d_l = move(dcontext, l_swap)
    rows = [pltpu.VMEM((128, 1024), BF16)]
    grad_chip = call(
        grad_chip_body, shape(128, 1024), [VM] * 3, dcontext, move(dcontext, other_core), context_weight,
        scratch=rows, flops=1 << 28, nbytes=3 << 20,
    )
    grad = call(
        grad_body, shape(256, 1024), [VM] * 4, grad_chip, d_l, move(d_l, other_core), context_weight,
        scratch=rows, flops=1 << 28, nbytes=3 << 20,
    )
    return losses.reshape(64), grad


def solution(mesh):
    fine = Mesh(mesh.devices.reshape(SIZES), AXES)
    seq, tp = AXES[:3], AXES[3:]
    return jax.shard_map(
        per_device,
        mesh=fine,
        in_specs=(
            P(seq, tp), P(seq, tp), P(seq, tp), P(seq, tp), P(tp, None), P(tp, None), P(seq + tp, None), P(), P(),
        ),
        out_specs=(P(seq + tp), P(seq, tp)),
        check_vma=False,
    )
```

```python
import functools
import itertools

import jax
import jax.numpy as jnp
from jax import lax
from jax.experimental import pallas as pl
from jax.experimental.pallas import tpu as pltpu
from jax.sharding import Mesh, PartitionSpec as P

HD = 128
DHEADS = 16
F32 = jnp.float32
BF16 = jnp.bfloat16
AXES = ("h", "x", "z", "l", "c")
SIZES = (2, 4, 4, 2, 2)
LOG2E = 1.4426950408889634
NEG = -1e30
VM = pl.BlockSpec(memory_space=pltpu.VMEM)
ANY = pl.BlockSpec(memory_space=pl.ANY)


def flat(coords):
    number = 0
    for coord, size in zip(coords, SIZES):
        number = number * size + coord
    return number


def move(array, target):
    pairs = []
    for coords in itertools.product(*map(range, SIZES)):
        pairs.append((flat(coords), flat(target(*coords))))
    return lax.ppermute(array, AXES, pairs)


def other_core(h, x, z, l, c):
    return h, x, z, l, 1 - c


def x_up(h, x, z, l, c):
    return h, (x + 1) % 4, z, l, c


def z_by(n):
    return lambda h, x, z, l, c: (h, x, (z + n) % 4, l, c)


def x_down(h, x, z, l, c):
    return h, (x + 3) % 4, z, l, c


def l_swap(h, x, z, l, c):
    return h, x, z, 1 - l, c


def call(body, out_shape, in_specs, *args, after=(), scratch=(), limit=16, flops=0, nbytes=0, aliases=None, out_specs=None):
    if out_specs is None:
        out_specs = jax.tree.map(lambda _: VM, out_shape)
    reads = len(args)

    def run(*refs):
        body(*refs[:reads], *refs[reads + len(after) :])

    args = args + tuple(after)
    in_specs = in_specs + [ANY] * len(after)
    return pl.pallas_call(
        run,
        out_shape=out_shape,
        in_specs=in_specs,
        out_specs=out_specs,
        scratch_shapes=list(scratch),
        input_output_aliases=aliases or {},
        compiler_params=pltpu.CompilerParams(vmem_limit_bytes=limit * 1024 * 1024),
        cost_estimate=pl.CostEstimate(flops=flops, bytes_accessed=nbytes, transcendentals=0),
    )(*args)


def shape(*dims, dtype=BF16):
    return jax.ShapeDtypeStruct(dims, dtype)


def dot_nn(a, b):
    return lax.dot_general(a, b, (((1,), (0,)), ((), ())), preferred_element_type=F32)


def dot_nt(a, b):
    return lax.dot_general(a, b, (((1,), (1,)), ((), ())), preferred_element_type=F32)


def dot_tn(a, b):
    return lax.dot_general(a, b, (((0,), (0,)), ((), ())), preferred_element_type=F32)


def split_rows_body(q_hbm, k_hbm, v_hbm, w_hbm, keep_ref, send_ref, cols_ref, local, sems):
    c = lax.axis_index("c")
    copies = [pltpu.make_async_copy(ref, local.at[n], sems.at[n]) for n, ref in enumerate((q_hbm, k_hbm, v_hbm))]
    cols = pl.ds(pl.multiple_of(lax.axis_index("z") * 256, 256), 256)
    copies.append(pltpu.make_async_copy(w_hbm.at[:, cols], cols_ref, sems.at[3]))
    for copy in copies:
        copy.start()
    for part in range(3):
        copies[part].wait()
        for half in range(2):
            mine = pl.ds(pl.multiple_of(half * 128 + c * 64, 64), 64)
            theirs = pl.ds(pl.multiple_of(half * 128 + (1 - c) * 64, 64), 64)
            for head in range(4):
                cols = slice(head * 128, head * 128 + 128)
                to = slice(part * 128, part * 128 + 128)
                keep_ref[c * 4 + head, half * 64 : half * 64 + 64, to] = local[part, mine, cols]
                send_ref[head, half * 64 : half * 64 + 64, to] = local[part, theirs, cols]
    copies[3].wait()


def attend(state, q, keys, vals_t, start, mask=None):
    acc_ref, m_ref, l_ref = state
    for first in range(0, 512, 128):
        cols = slice(start + first, start + first + 128)
        s = dot_nt(keys, q[first : first + 128]) * (LOG2E / HD**0.5)
        if mask is not None:
            s = jnp.where(mask[:, first : first + 128], s, NEG)
        old = m_ref[:, cols]
        new = jnp.maximum(old, jnp.max(s, 0, keepdims=True))
        p = jnp.exp2(s - new)
        alpha = jnp.exp2(old - new)
        m_ref[:, cols] = new
        l_ref[:, cols] = l_ref[:, cols] * alpha + jnp.sum(p, 0, keepdims=True)
        acc_ref[:, cols] = acc_ref[:, cols] * alpha + dot_nn(vals_t, p.astype(BF16))


def rows_of(ref, first):
    return ref[first : first + 4, :, 0:128].reshape(512, 128)


def values_of(ref, first):
    return jnp.concatenate([ref[first + n, :, 128:256] for n in range(4)], 1)


def take_rows_body(r_ref, lo_ref, hi_ref, q_ref):
    q_ref[...] = r_ref[:, :, 0:128]
    for n in range(8):
        ref = lo_ref if n < 4 else hi_ref
        ref[n % 4, :, 0:128] = r_ref[n, :, 128:256]
        ref[n % 4, :, 128:256] = r_ref[n, :, 256:384].T


def carry_over(ins, outs):
    for source, target in zip(ins, outs):
        target[...] = source[...]
    return outs


def own_block_body(q_ref, q_o_ref, lo_in, hi_in, w_in, acc_ref, m_ref, l_ref, w_ref):
    w_ref[...] = w_in[...]
    state = (acc_ref, m_ref, l_ref)
    c = lax.axis_index("c")
    m_ref[...] = jnp.full_like(m_ref, 0.1 * NEG)
    l_ref[...] = jnp.zeros_like(l_ref)
    acc_ref[...] = jnp.zeros_like(acc_ref)
    key_row = lax.broadcasted_iota(jnp.int32, (512, 512), 0)
    q_row = lax.broadcasted_iota(jnp.int32, (512, 512), 1)
    place = lambda row, core: (row // 64) * 128 + core * 64 + row % 64
    key_place = place(key_row, c)
    for section, (ref, core) in enumerate(((q_ref, c), (q_o_ref, 1 - c))):
        mask = key_place <= place(q_row, core)
        for h, kv in enumerate((lo_in, hi_in)):
            attend(state, rows_of(ref, h * 4), rows_of(kv, 0), values_of(kv, 0), h * 1024 + section * 512, mask)
        attend(state, rows_of(ref, 4), rows_of(lo_in, 0), values_of(lo_in, 0), 1024 + section * 512)


def low_step(state, qs, kv, earlier):
    for section, ref in enumerate(qs):
        attend(state, rows_of(ref, 4), rows_of(kv, 0), values_of(kv, 0), 1024 + section * 512)

    @pl.when(earlier)
    def _():
        for section, ref in enumerate(qs):
            attend(state, rows_of(ref, 0), rows_of(kv, 0), values_of(kv, 0), section * 512)


def high_step(state, qs, kv, earlier):
    @pl.when(earlier)
    def _():
        for section, ref in enumerate(qs):
            attend(state, rows_of(ref, 4), rows_of(kv, 0), values_of(kv, 0), 1024 + section * 512)


def first_blocks_body(
    q_ref, q_o_ref, up_lo, down_hi, low, high, acc_in, m_in, l_in, acc_ref, m_ref, l_ref, lo_ref, hi_ref
):
    carry_over((low, high), (lo_ref, hi_ref))
    state = carry_over((acc_in, m_in, l_in), (acc_ref, m_ref, l_ref))
    x = lax.axis_index("x")
    low_step(state, (q_ref, q_o_ref), up_lo, x > 0)
    high_step(state, (q_ref, q_o_ref), down_hi, x == 3)


def far_blocks_body(q_ref, q_o_ref, lo, hi, acc_in, m_in, l_in, acc_ref, m_ref, l_ref):
    state = carry_over((acc_in, m_in, l_in), (acc_ref, m_ref, l_ref))
    earlier = lax.axis_index("x") >= 2
    low_step(state, (q_ref, q_o_ref), lo, earlier)
    high_step(state, (q_ref, q_o_ref), hi, earlier)


def last_blocks_body(
    q_ref, q_o_ref, up_hi, down_lo, acc_in, m_in, l_in, own_ref, send_ref, own_stat, acc_ref, m_ref, l_ref
):
    state = carry_over((acc_in, m_in, l_in), (acc_ref, m_ref, l_ref))
    x = lax.axis_index("x")
    high_step(state, (q_ref, q_o_ref), up_hi, x > 0)
    low_step(state, (q_ref, q_o_ref), down_lo, x == 3)
    send_ref[...] = jnp.zeros_like(send_ref)
    for section in range(2):
        for h in range(2):
            cols = slice(h * 1024 + section * 512, h * 1024 + section * 512 + 512)
            to = slice(h * 512, h * 512 + 512)
            top = m_ref[:, cols]
            total = l_ref[:, cols]
            part = acc_ref[:, cols] / jnp.maximum(total, 0.5)
            if section == 0:
                own_ref[:, to] = part
                own_stat[0:1, to] = top
                own_stat[1:2, to] = total
            else:
                send_ref[0:128, to] = part.astype(BF16)
                for n, value in enumerate((top, total)):
                    for term in range(3):
                        piece = value.astype(BF16)
                        send_ref[128 + n * 16 + term : 129 + n * 16 + term, to] = piece
                        value = value - piece.astype(F32)


def join_cores_body(own_ref, recv_ref, own_stat, out_ref):
    m1, l1 = own_stat[0:1, :], own_stat[1:2, :]
    stat = recv_ref[128:160, :].astype(F32)
    m2 = stat[0:1] + stat[1:2] + stat[2:3]
    l2 = stat[16:17] + stat[17:18] + stat[18:19]
    top = jnp.maximum(m1, m2)
    w1 = l1 * jnp.exp2(m1 - top)
    w2 = l2 * jnp.exp2(m2 - top)
    share = 1.0 / (w1 + w2)
    joined = own_ref[...] * (w1 * share) + recv_ref[0:128, :].astype(F32) * (w2 * share)
    out_ref[...] = joined.T.astype(BF16).reshape(8, 128, 128)


def merged_weight_body(ow_ref, b00, b01, b10, b11, out_ref):
    l, c = lax.axis_index("l"), lax.axis_index("c")
    total = None
    for dl, dc, ref in ((0, 0, b00), (0, 1, b01), (1, 0, b10), (1, 1, b11)):
        t = jnp.where(dl == 1, 1 - l, l) * 2 + jnp.where(dc == 1, 1 - c, c)
        part = dot_nn(ow_ref[:, pl.ds(pl.multiple_of(t * 1024, 1024), 1024)], ref[...])
        total = part if total is None else total + part
    out_ref[...] = total.astype(BF16)


def hidden_part_body(hid_ref, cw_ref, own_ref, send_ref, out):
    c = lax.axis_index("c")
    out[...] = dot_nn(hid_ref[...], cw_ref[...])
    for half in range(2):
        rows = slice(half * 64, half * 64 + 64)
        own_ref[rows, :] = out[pl.ds(pl.multiple_of(half * 128 + c * 64, 64), 64), :]
        send_ref[rows, :] = out[pl.ds(pl.multiple_of(half * 128 + (1 - c) * 64, 64), 64), :].astype(BF16)


def embed_body(codes_ref, table_ref, out_ref):
    vocab = lax.broadcasted_iota(jnp.int32, (64, 1024), 1)
    for n in range(3):
        hit = (vocab == codes_ref[:, n : n + 1]).astype(BF16)
        out_ref[n] = dot_nn(hit, table_ref[n]).astype(BF16)


def relay_body(lo_in, hi_in, lo_ref, hi_ref):
    carry_over((lo_in, hi_in), (lo_ref, hi_ref))


def pack_body(*refs):
    for n in range(4):
        refs[4][n] = refs[n][...]


def project_body(att_ref, w_ref, wo_ref, h_own_ref, h_recv_ref, own_ref, send_ref, out):
    z, l, c = lax.axis_index("z"), lax.axis_index("l"), lax.axis_index("c")
    a_own = att_ref[pl.ds(c * 4, 4)]
    a_oth = att_ref[pl.ds((1 - c) * 4, 4)]
    a_own = jnp.concatenate([a_own[i] for i in range(4)], 1)
    a_oth = jnp.concatenate([a_oth[i] for i in range(4)], 1)
    for dz in range(4):
        col = pl.multiple_of(((z + 4 - dz) % 4) * 256, 256)
        out[:, pl.ds(col, 256)] = dot_nn(a_own, w_ref[dz]) + dot_nn(a_oth, wo_ref[dz])
    out[...] += h_own_ref[...] + h_recv_ref[...].astype(F32)
    own_ref[...] = out[pl.ds(pl.multiple_of(l * 64, 64), 64), :]
    send_ref[...] = out[pl.ds(pl.multiple_of((1 - l) * 64, 64), 64), :].astype(BF16)


def rms(stream):
    return lax.rsqrt(jnp.mean(stream * stream, -1, keepdims=True) + 1e-05)


def depth_body(
    own_ref, recv_ref, embed_ref, codes_ref, wt_hbm, tab_hbm, loss_ref, dctx_ref, wt, tab, sems,
):
    copies = [pltpu.make_async_copy(wt_hbm.at[i], wt.at[i], sems.at[i]) for i in range(4)]
    copies += [pltpu.make_async_copy(tab_hbm.at[i], tab.at[i], sems.at[4 + i]) for i in range(4)]
    for copy in copies:
        copy.start()
    n = 64
    context = own_ref[...] + recv_ref[...].astype(F32)
    stream = jnp.concatenate([context] + [context + embed_ref[i].astype(F32) for i in range(3)], 0)
    r1 = rms(stream)
    normed = (stream * r1).astype(BF16)
    qkv = []
    for i in range(3):
        copies[i].wait()
        qkv.append(dot_nn(normed, wt[i]))
    q, k, v = qkv
    at = lambda a, i: a[i * n : (i + 1) * n]
    pairs = [(i, j) for i in range(1, 4) for j in range(i + 1)]
    lane = lax.broadcasted_iota(jnp.int32, (1024, 128), 0) // 64
    head = lax.broadcasted_iota(jnp.int32, (1024, 128), 1)
    gather_heads = (lane == head).astype(BF16)
    head_t = lax.broadcasted_iota(jnp.int32, (128, 1024), 0)
    lane_t = lax.broadcasted_iota(jnp.int32, (128, 1024), 1) // 64
    spread_heads = (lane_t == head_t).astype(BF16)
    prod = jnp.concatenate([at(q, i) * at(k, j) for i, j in pairs], 0)
    scores = dot_nn(prod.astype(BF16), gather_heads) * 0.125
    score = {pair: at(scores, number) for number, pair in enumerate(pairs)}
    weight = {}
    for i in range(1, 4):
        top = functools.reduce(jnp.maximum, [score[i, j] for j in range(i + 1)])
        es = [jnp.exp(score[i, j] - top) for j in range(i + 1)]
        total = functools.reduce(jnp.add, es)
        for j in range(i + 1):
            weight[i, j] = es[j] / total
    spread = dot_nn(jnp.concatenate([weight[p] for p in pairs], 0).astype(BF16), spread_heads)
    wide = {pair: at(spread, number) for number, pair in enumerate(pairs)}
    mixed = jnp.concatenate(
        [at(v, 0)] + [functools.reduce(jnp.add, [wide[i, j] * at(v, j) for j in range(i + 1)]) for i in range(1, 4)], 0
    ).astype(BF16)
    copies[3].wait()
    update = dot_nn(mixed, wt[3])
    out = stream + update
    r2 = rms(out)
    final = (out * r2).astype(BF16)
    scale = 3.0 / 1024**0.5
    logits = []
    for i in range(4):
        copies[4 + i].wait()
    for i in range(4):
        logits.append(dot_nt(at(final, i), tab[i]))
    logits = jnp.concatenate(logits, 0) * scale
    top = jnp.max(logits, -1, keepdims=True)
    e = jnp.exp(logits - top)
    total = jnp.sum(e, -1, keepdims=True)
    vocab = lax.broadcasted_iota(jnp.int32, (4 * n, 1024), 1)
    hit = vocab == jnp.concatenate([codes_ref[:, i : i + 1] for i in range(4)], 0)
    picked = jnp.sum(jnp.where(hit, logits, 0.0), -1, keepdims=True)
    losses = top + jnp.log(total) - picked
    loss = functools.reduce(jnp.add, [at(losses, i) for i in range(4)])
    loss_ref[...] = jnp.broadcast_to(loss, (n, 128)).T[0:1, :]
    dlogits = (e * (1.0 / total) - hit.astype(F32)).astype(BF16)
    dfinal = [dot_nn(at(dlogits, i), tab[i]) * scale for i in range(4)]
    dfinal = jnp.concatenate(dfinal, 0)
    dout = r2 * (dfinal - out * (r2 * r2) * jnp.mean(dfinal * out, -1, keepdims=True))
    dmixed = dot_nt(dout.astype(BF16), wt[3])
    dprod = jnp.concatenate([at(dmixed, i) * at(v, j) for i, j in pairs], 0)
    dweights = dot_nn(dprod.astype(BF16), gather_heads)
    dweight = {pair: at(dweights, number) for number, pair in enumerate(pairs)}
    dscore = []
    for i in range(1, 4):
        mean = functools.reduce(jnp.add, [weight[i, j] * dweight[i, j] for j in range(i + 1)])
        for j in range(i + 1):
            dscore.append(weight[i, j] * (dweight[i, j] - mean) * 0.125)
    spread = dot_nn(jnp.concatenate(dscore, 0).astype(BF16), spread_heads)
    dwide = {pair: at(spread, number) for number, pair in enumerate(pairs)}
    add = lambda terms: functools.reduce(jnp.add, terms)
    dq = [add([dwide[i, j] * at(k, j) for j in range(i + 1)]) for i in range(1, 4)]
    dq = jnp.concatenate([jnp.zeros((n, 1024), F32)] + dq, 0)
    dk = jnp.concatenate([add([dwide[i, j] * at(q, i) for i in range(max(j, 1), 4)]) for j in range(4)], 0)
    dv = [add([wide[i, j] * at(dmixed, i) for i in range(max(j, 1), 4)]) for j in range(4)]
    dv = jnp.concatenate([dv[0] + at(dmixed, 0)] + dv[1:], 0)
    dnormed = dot_nt(dq.astype(BF16), wt[0]) + dot_nt(dk.astype(BF16), wt[1]) + dot_nt(dv.astype(BF16), wt[2])
    dstream = dout + r1 * (dnormed - stream * (r1 * r1) * jnp.mean(dnormed * stream, -1, keepdims=True))
    dctx_ref[...] = add([at(dstream, i) for i in range(4)]).astype(BF16)


def grad_chip_body(own_ref, other_ref, cw_ref, out_ref, rows):
    c = lax.axis_index("c")
    rows[pl.ds(pl.multiple_of(c * 64, 64), 64), :] = own_ref[...]
    rows[pl.ds(pl.multiple_of((1 - c) * 64, 64), 64), :] = other_ref[...]
    out_ref[...] = dot_nt(rows[...], cw_ref[...]).astype(BF16)


def grad_body(chip_ref, l_ref, lc_ref, cw_ref, out_ref, rows):
    l, c = lax.axis_index("l"), lax.axis_index("c")
    rows[pl.ds(pl.multiple_of(c * 64, 64), 64), :] = l_ref[...]
    rows[pl.ds(pl.multiple_of((1 - c) * 64, 64), 64), :] = lc_ref[...]
    out_ref[pl.ds(pl.multiple_of(l * 128, 128), 128), :] = chip_ref[...]
    out_ref[pl.ds(pl.multiple_of((1 - l) * 128, 128), 128), :] = dot_nt(rows[...], cw_ref[...]).astype(BF16)


def per_device(hidden_in, queries, keys, values, out_weight, context_weight, codes, table, depth_weights):
    c = lax.axis_index("c")

    keep, send, cw_cols = call(
        split_rows_body, (shape(8, 128, 384), shape(4, 128, 384), shape(1024, 256)), [ANY] * 4,
        queries, keys, values, context_weight,
        scratch=[pltpu.VMEM((3, 256, 512), BF16), pltpu.SemaphoreType.DMA((4,))], limit=60, nbytes=3 << 20,
    )
    full = lax.dynamic_update_slice(keep, move(send, other_core), ((1 - c) * 4, 0, 0))
    mine = lax.all_to_all(full, ("h", "z"), 0, 0, tiled=True)

    cw_l = move(cw_cols, l_swap)
    cw_c = move(cw_cols, other_core)
    cw_lc = move(cw_l, other_core)
    h_own, h_send = call(
        hidden_part_body, (shape(128, 1024, dtype=F32), shape(128, 1024)), [VM] * 2,
        hidden_in, context_weight, scratch=[pltpu.VMEM((256, 1024), F32)], flops=1 << 29, nbytes=3 << 20,
    )
    merged = call(
        merged_weight_body, shape(512, 256), [VM] * 5, out_weight, cw_cols, cw_c, cw_l, cw_lc,
        flops=1 << 30, nbytes=6 << 20,
    )
    half = shape(4, 128, 256)
    low, high, q = call(
        take_rows_body, (half, half, shape(8, 128, 128)), [VM], mine, after=(h_own, merged), nbytes=1 << 20
    )
    up_lo, down_hi = move(low, x_up), move(high, x_down)
    q_o = move(q, other_core)
    stats = (shape(128, 2048, dtype=F32), shape(1, 2048, dtype=F32), shape(1, 2048, dtype=F32))
    *carry, merged = call(
        own_block_body, stats + (shape(512, 256),), [VM] * 5, q, q_o, low, high, merged, flops=4 << 30, nbytes=2 << 20
    )
    pieces = [merged] + [move(merged, z_by(n)) for n in (1, 2, 3)]
    relay_lo, relay_hi = call(relay_body, (half, half), [VM] * 2, up_lo, down_hi, after=carry[1:2], nbytes=1 << 20)
    far_lo, far_hi = move(relay_lo, x_up), move(relay_hi, x_down)
    *carry, low, high = call(
        first_blocks_body, stats + (half, half), [VM] * 9, q, q_o, up_lo, down_hi, low, high, *carry, after=(relay_lo,),
        aliases={6: 0, 7: 1, 8: 2}, flops=3 << 30, nbytes=4 << 20,
    )
    up_hi, down_lo = move(high, x_up), move(low, x_down)
    carry = call(
        far_blocks_body, stats, [VM] * 7, q, q_o, far_lo, far_hi, *carry,
        aliases={4: 0, 5: 1, 6: 2}, flops=3 << 30, nbytes=3 << 20,
    )
    h_recv = move(h_send, other_core)
    embedded = call(embed_body, shape(3, 64, 1024), [VM] * 2, codes, table, after=carry[1:2], flops=3 << 27, nbytes=8 << 20)
    own, send, own_stat = call(
        last_blocks_body, (shape(128, 1024, dtype=F32), shape(160, 1024), shape(8, 1024, dtype=F32)),
        [VM] * 7, q, q_o, up_hi, down_lo, *carry, after=(embedded, h_recv, *pieces[1:]),
        scratch=[pltpu.VMEM(s.shape, s.dtype) for s in stats], flops=3 << 30, nbytes=3 << 20,
    )
    joined = move(send, other_core)
    attended = call(join_cores_body, shape(8, 128, 128), [VM] * 3, own, joined, own_stat, nbytes=1 << 20)
    merged = call(pack_body, shape(4, 512, 256), [VM] * 4, *pieces, after=(joined,), nbytes=2 << 20)
    merged_o = move(merged, other_core)
    attended = lax.all_to_all(attended, ("h", "z"), 0, 0, tiled=True)

    own, send = call(
        project_body, (shape(64, 1024, dtype=F32), shape(64, 1024)), [VM] * 5,
        attended, merged, merged_o, h_own, h_recv,
        scratch=[pltpu.VMEM((128, 1024), F32)], flops=1 << 28, nbytes=3 << 20,
    )
    recv = move(send, l_swap)
    losses, dcontext = call(
        depth_body, (shape(1, 64, dtype=F32), shape(64, 1024)), [VM] * 4 + [ANY] * 2,
        own, recv, embedded, codes, depth_weights, table,
        scratch=[pltpu.VMEM((4, 1024, 1024), BF16), pltpu.VMEM((4, 1024, 1024), BF16), pltpu.SemaphoreType.DMA((8,))],
        limit=60, flops=12 << 30, nbytes=17 << 20,
    )
    d_l = move(dcontext, l_swap)
    rows = [pltpu.VMEM((128, 1024), BF16)]
    grad_chip = call(
        grad_chip_body, shape(128, 1024), [VM] * 3, dcontext, move(dcontext, other_core), context_weight,
        scratch=rows, flops=1 << 28, nbytes=3 << 20,
    )
    grad = call(
        grad_body, shape(256, 1024), [VM] * 4, grad_chip, d_l, move(d_l, other_core), context_weight,
        scratch=rows, flops=1 << 28, nbytes=3 << 20,
    )
    return losses.reshape(64), grad


def solution(mesh):
    fine = Mesh(mesh.devices.reshape(SIZES), AXES)
    seq, tp = AXES[:3], AXES[3:]
    return jax.shard_map(
        per_device,
        mesh=fine,
        in_specs=(
            P(seq, tp), P(seq, tp), P(seq, tp), P(seq, tp), P(tp, None), P(tp, None), P(seq + tp, None), P(), P(),
        ),
        out_specs=(P(seq + tp), P(seq, tp)),
        check_vma=False,
    )
```

```python
import functools
import itertools

import jax
import jax.numpy as jnp
from jax import lax
from jax.experimental import pallas as pl
from jax.experimental.pallas import tpu as pltpu
from jax.sharding import Mesh, PartitionSpec as P

HD = 128
DHEADS = 16
F32 = jnp.float32
BF16 = jnp.bfloat16
AXES = ("h", "x", "z", "l", "c")
SIZES = (2, 4, 4, 2, 2)
LOG2E = 1.4426950408889634
NEG = -1e30
VM = pl.BlockSpec(memory_space=pltpu.VMEM)
ANY = pl.BlockSpec(memory_space=pl.ANY)


def flat(coords):
    number = 0
    for coord, size in zip(coords, SIZES):
        number = number * size + coord
    return number


def move(array, target):
    pairs = []
    for coords in itertools.product(*map(range, SIZES)):
        pairs.append((flat(coords), flat(target(*coords))))
    return lax.ppermute(array, AXES, pairs)


def other_core(h, x, z, l, c):
    return h, x, z, l, 1 - c


def x_up(h, x, z, l, c):
    return h, (x + 1) % 4, z, l, c


def z_by(n):
    return lambda h, x, z, l, c: (h, x, (z + n) % 4, l, c)


def x_down(h, x, z, l, c):
    return h, (x + 3) % 4, z, l, c


def l_swap(h, x, z, l, c):
    return h, x, z, 1 - l, c


def call(body, out_shape, in_specs, *args, after=(), scratch=(), limit=16, flops=0, nbytes=0, aliases=None, out_specs=None):
    if out_specs is None:
        out_specs = jax.tree.map(lambda _: VM, out_shape)
    reads = len(args)

    def run(*refs):
        body(*refs[:reads], *refs[reads + len(after) :])

    args = args + tuple(after)
    in_specs = in_specs + [ANY] * len(after)
    return pl.pallas_call(
        run,
        out_shape=out_shape,
        in_specs=in_specs,
        out_specs=out_specs,
        scratch_shapes=list(scratch),
        input_output_aliases=aliases or {},
        compiler_params=pltpu.CompilerParams(vmem_limit_bytes=limit * 1024 * 1024),
        cost_estimate=pl.CostEstimate(flops=flops, bytes_accessed=nbytes, transcendentals=0),
    )(*args)


def shape(*dims, dtype=BF16):
    return jax.ShapeDtypeStruct(dims, dtype)


def dot_nn(a, b):
    return lax.dot_general(a, b, (((1,), (0,)), ((), ())), preferred_element_type=F32)


def dot_nt(a, b):
    return lax.dot_general(a, b, (((1,), (1,)), ((), ())), preferred_element_type=F32)


def dot_tn(a, b):
    return lax.dot_general(a, b, (((0,), (0,)), ((), ())), preferred_element_type=F32)


def split_rows_body(q_hbm, k_hbm, v_hbm, w_hbm, keep_ref, send_ref, cols_ref, local, sems):
    c = lax.axis_index("c")
    copies = [pltpu.make_async_copy(ref, local.at[n], sems.at[n]) for n, ref in enumerate((q_hbm, k_hbm, v_hbm))]
    cols = pl.ds(pl.multiple_of(lax.axis_index("z") * 256, 256), 256)
    copies.append(pltpu.make_async_copy(w_hbm.at[:, cols], cols_ref, sems.at[3]))
    for copy in copies:
        copy.start()
    for part in range(3):
        copies[part].wait()
        for half in range(2):
            mine = pl.ds(pl.multiple_of(half * 128 + c * 64, 64), 64)
            theirs = pl.ds(pl.multiple_of(half * 128 + (1 - c) * 64, 64), 64)
            for head in range(4):
                cols = slice(head * 128, head * 128 + 128)
                to = slice(part * 128, part * 128 + 128)
                keep_ref[c * 4 + head, half * 64 : half * 64 + 64, to] = local[part, mine, cols]
                send_ref[head, half * 64 : half * 64 + 64, to] = local[part, theirs, cols]
    copies[3].wait()


def attend(state, q, keys, vals_t, start, mask=None):
    acc_ref, m_ref, l_ref = state
    for first in range(0, 512, 128):
        cols = slice(start + first, start + first + 128)
        s = dot_nt(keys, q[first : first + 128]) * (LOG2E / HD**0.5)
        if mask is not None:
            s = jnp.where(mask[:, first : first + 128], s, NEG)
        old = m_ref[:, cols]
        new = jnp.maximum(old, jnp.max(s, 0, keepdims=True))
        p = jnp.exp2(s - new)
        alpha = jnp.exp2(old - new)
        m_ref[:, cols] = new
        l_ref[:, cols] = l_ref[:, cols] * alpha + jnp.sum(p, 0, keepdims=True)
        acc_ref[:, cols] = acc_ref[:, cols] * alpha + dot_nn(vals_t, p.astype(BF16))


def rows_of(ref, first):
    return ref[first : first + 4, :, 0:128].reshape(512, 128)


def values_of(ref, first):
    return jnp.concatenate([ref[first + n, :, 128:256] for n in range(4)], 1)


def take_rows_body(r_ref, lo_ref, hi_ref, q_ref):
    q_ref[...] = r_ref[:, :, 0:128]
    for n in range(8):
        ref = lo_ref if n < 4 else hi_ref
        ref[n % 4, :, 0:128] = r_ref[n, :, 128:256]
        ref[n % 4, :, 128:256] = r_ref[n, :, 256:384].T


def carry_over(ins, outs):
    for source, target in zip(ins, outs):
        target[...] = source[...]
    return outs


def own_block_body(q_ref, q_o_ref, lo_in, hi_in, w_in, acc_ref, m_ref, l_ref, w_ref):
    w_ref[...] = w_in[...]
    state = (acc_ref, m_ref, l_ref)
    c = lax.axis_index("c")
    m_ref[...] = jnp.full_like(m_ref, 0.1 * NEG)
    l_ref[...] = jnp.zeros_like(l_ref)
    acc_ref[...] = jnp.zeros_like(acc_ref)
    key_row = lax.broadcasted_iota(jnp.int32, (512, 512), 0)
    q_row = lax.broadcasted_iota(jnp.int32, (512, 512), 1)
    place = lambda row, core: (row // 64) * 128 + core * 64 + row % 64
    key_place = place(key_row, c)
    for section, (ref, core) in enumerate(((q_ref, c), (q_o_ref, 1 - c))):
        mask = key_place <= place(q_row, core)
        for h, kv in enumerate((lo_in, hi_in)):
            attend(state, rows_of(ref, h * 4), rows_of(kv, 0), values_of(kv, 0), h * 1024 + section * 512, mask)
        attend(state, rows_of(ref, 4), rows_of(lo_in, 0), values_of(lo_in, 0), 1024 + section * 512)


def low_step(state, qs, kv, earlier):
    for section, ref in enumerate(qs):
        attend(state, rows_of(ref, 4), rows_of(kv, 0), values_of(kv, 0), 1024 + section * 512)

    @pl.when(earlier)
    def _():
        for section, ref in enumerate(qs):
            attend(state, rows_of(ref, 0), rows_of(kv, 0), values_of(kv, 0), section * 512)


def high_step(state, qs, kv, earlier):
    @pl.when(earlier)
    def _():
        for section, ref in enumerate(qs):
            attend(state, rows_of(ref, 4), rows_of(kv, 0), values_of(kv, 0), 1024 + section * 512)


def first_blocks_body(
    q_ref, q_o_ref, up_lo, down_hi, low, high, acc_in, m_in, l_in, acc_ref, m_ref, l_ref, lo_ref, hi_ref
):
    carry_over((low, high), (lo_ref, hi_ref))
    state = carry_over((acc_in, m_in, l_in), (acc_ref, m_ref, l_ref))
    x = lax.axis_index("x")
    low_step(state, (q_ref, q_o_ref), up_lo, x > 0)
    high_step(state, (q_ref, q_o_ref), down_hi, x == 3)


def far_blocks_body(q_ref, q_o_ref, lo, hi, acc_in, m_in, l_in, acc_ref, m_ref, l_ref):
    state = carry_over((acc_in, m_in, l_in), (acc_ref, m_ref, l_ref))
    earlier = lax.axis_index("x") >= 2
    low_step(state, (q_ref, q_o_ref), lo, earlier)
    high_step(state, (q_ref, q_o_ref), hi, earlier)


def last_blocks_body(
    q_ref, q_o_ref, up_hi, down_lo, acc_in, m_in, l_in, own_ref, send_ref, own_stat, acc_ref, m_ref, l_ref
):
    state = carry_over((acc_in, m_in, l_in), (acc_ref, m_ref, l_ref))
    x = lax.axis_index("x")
    high_step(state, (q_ref, q_o_ref), up_hi, x > 0)
    low_step(state, (q_ref, q_o_ref), down_lo, x == 3)
    send_ref[...] = jnp.zeros_like(send_ref)
    for section in range(2):
        for h in range(2):
            cols = slice(h * 1024 + section * 512, h * 1024 + section * 512 + 512)
            to = slice(h * 512, h * 512 + 512)
            top = m_ref[:, cols]
            total = l_ref[:, cols]
            part = acc_ref[:, cols] / jnp.maximum(total, 0.5)
            if section == 0:
                own_ref[:, to] = part
                own_stat[0:1, to] = top
                own_stat[1:2, to] = total
            else:
                send_ref[0:128, to] = part.astype(BF16)
                for n, value in enumerate((top, total)):
                    for term in range(3):
                        piece = value.astype(BF16)
                        send_ref[128 + n * 16 + term : 129 + n * 16 + term, to] = piece
                        value = value - piece.astype(F32)


def join_cores_body(own_ref, recv_ref, own_stat, out_ref):
    m1, l1 = own_stat[0:1, :], own_stat[1:2, :]
    stat = recv_ref[128:160, :].astype(F32)
    m2 = stat[0:1] + stat[1:2] + stat[2:3]
    l2 = stat[16:17] + stat[17:18] + stat[18:19]
    top = jnp.maximum(m1, m2)
    w1 = l1 * jnp.exp2(m1 - top)
    w2 = l2 * jnp.exp2(m2 - top)
    share = 1.0 / (w1 + w2)
    joined = own_ref[...] * (w1 * share) + recv_ref[0:128, :].astype(F32) * (w2 * share)
    out_ref[...] = joined.T.astype(BF16).reshape(8, 128, 128)


def merged_weight_body(ow_ref, b00, b01, b10, b11, out_ref):
    l, c = lax.axis_index("l"), lax.axis_index("c")
    total = None
    for dl, dc, ref in ((0, 0, b00), (0, 1, b01), (1, 0, b10), (1, 1, b11)):
        t = jnp.where(dl == 1, 1 - l, l) * 2 + jnp.where(dc == 1, 1 - c, c)
        part = dot_nn(ow_ref[:, pl.ds(pl.multiple_of(t * 1024, 1024), 1024)], ref[...])
        total = part if total is None else total + part
    out_ref[...] = total.astype(BF16)


def hidden_part_body(hid_ref, cw_ref, own_ref, send_ref, out):
    c = lax.axis_index("c")
    out[...] = dot_nn(hid_ref[...], cw_ref[...])
    for half in range(2):
        rows = slice(half * 64, half * 64 + 64)
        own_ref[rows, :] = out[pl.ds(pl.multiple_of(half * 128 + c * 64, 64), 64), :]
        send_ref[rows, :] = out[pl.ds(pl.multiple_of(half * 128 + (1 - c) * 64, 64), 64), :].astype(BF16)


def embed_body(codes_ref, table_ref, out_ref):
    vocab = lax.broadcasted_iota(jnp.int32, (64, 1024), 1)
    for n in range(3):
        hit = (vocab == codes_ref[:, n : n + 1]).astype(BF16)
        out_ref[n] = dot_nn(hit, table_ref[n]).astype(BF16)


def relay_body(lo_in, hi_in, lo_ref, hi_ref):
    carry_over((lo_in, hi_in), (lo_ref, hi_ref))


def pack_body(*refs):
    for n in range(4):
        refs[4][n] = refs[n][...]


def project_body(att_ref, w_ref, wo_ref, h_own_ref, h_recv_ref, own_ref, send_ref, out):
    z, l, c = lax.axis_index("z"), lax.axis_index("l"), lax.axis_index("c")
    a_own = att_ref[pl.ds(c * 4, 4)]
    a_oth = att_ref[pl.ds((1 - c) * 4, 4)]
    a_own = jnp.concatenate([a_own[i] for i in range(4)], 1)
    a_oth = jnp.concatenate([a_oth[i] for i in range(4)], 1)
    for dz in range(4):
        col = pl.multiple_of(((z + 4 - dz) % 4) * 256, 256)
        out[:, pl.ds(col, 256)] = dot_nn(a_own, w_ref[dz]) + dot_nn(a_oth, wo_ref[dz])
    out[...] += h_own_ref[...] + h_recv_ref[...].astype(F32)
    own_ref[...] = out[pl.ds(pl.multiple_of(l * 64, 64), 64), :]
    send_ref[...] = out[pl.ds(pl.multiple_of((1 - l) * 64, 64), 64), :].astype(BF16)


def rms(stream):
    return lax.rsqrt(jnp.mean(stream * stream, -1, keepdims=True) + 1e-05)


def depth_body(
    own_ref, recv_ref, embed_ref, codes_ref, wt_hbm, tab_hbm, loss_ref, dctx_ref, wt, tab, sems,
):
    copies = [pltpu.make_async_copy(wt_hbm.at[i], wt.at[i], sems.at[i]) for i in range(4)]
    copies += [pltpu.make_async_copy(tab_hbm.at[i], tab.at[i], sems.at[4 + i]) for i in range(4)]
    for copy in copies:
        copy.start()
    n = 64
    context = own_ref[...] + recv_ref[...].astype(F32)
    stream = jnp.concatenate([context] + [context + embed_ref[i].astype(F32) for i in range(3)], 0)
    r1 = rms(stream)
    normed = (stream * r1).astype(BF16)
    qkv = []
    for i in range(3):
        copies[i].wait()
        qkv.append(dot_nn(normed, wt[i]))
    q, k, v = qkv
    at = lambda a, i: a[i * n : (i + 1) * n]
    pairs = [(i, j) for i in range(1, 4) for j in range(i + 1)]
    lane = lax.broadcasted_iota(jnp.int32, (1024, 128), 0) // 64
    head = lax.broadcasted_iota(jnp.int32, (1024, 128), 1)
    gather_heads = (lane == head).astype(BF16)
    head_t = lax.broadcasted_iota(jnp.int32, (128, 1024), 0)
    lane_t = lax.broadcasted_iota(jnp.int32, (128, 1024), 1) // 64
    spread_heads = (lane_t == head_t).astype(BF16)
    prod = jnp.concatenate([at(q, i) * at(k, j) for i, j in pairs], 0)
    scores = dot_nn(prod.astype(BF16), gather_heads) * 0.125
    score = {pair: at(scores, number) for number, pair in enumerate(pairs)}
    weight = {}
    for i in range(1, 4):
        top = functools.reduce(jnp.maximum, [score[i, j] for j in range(i + 1)])
        es = [jnp.exp(score[i, j] - top) for j in range(i + 1)]
        total = functools.reduce(jnp.add, es)
        for j in range(i + 1):
            weight[i, j] = es[j] / total
    spread = dot_nn(jnp.concatenate([weight[p] for p in pairs], 0).astype(BF16), spread_heads)
    wide = {pair: at(spread, number) for number, pair in enumerate(pairs)}
    mixed = jnp.concatenate(
        [at(v, 0)] + [functools.reduce(jnp.add, [wide[i, j] * at(v, j) for j in range(i + 1)]) for i in range(1, 4)], 0
    ).astype(BF16)
    copies[3].wait()
    update = dot_nn(mixed, wt[3])
    out = stream + update
    r2 = rms(out)
    final = (out * r2).astype(BF16)
    scale = 3.0 / 1024**0.5
    logits = []
    for i in range(4):
        copies[4 + i].wait()
    for i in range(4):
        logits.append(dot_nt(at(final, i), tab[i]))
    logits = jnp.concatenate(logits, 0) * scale
    top = jnp.max(logits, -1, keepdims=True)
    e = jnp.exp(logits - top)
    total = jnp.sum(e, -1, keepdims=True)
    vocab = lax.broadcasted_iota(jnp.int32, (4 * n, 1024), 1)
    hit = vocab == jnp.concatenate([codes_ref[:, i : i + 1] for i in range(4)], 0)
    picked = jnp.sum(jnp.where(hit, logits, 0.0), -1, keepdims=True)
    losses = top + jnp.log(total) - picked
    loss = functools.reduce(jnp.add, [at(losses, i) for i in range(4)])
    loss_ref[...] = jnp.broadcast_to(loss, (n, 128)).T[0:1, :]
    dlogits = (e * (1.0 / total) - hit.astype(F32)).astype(BF16)
    dfinal = [dot_nn(at(dlogits, i), tab[i]) * scale for i in range(4)]
    dfinal = jnp.concatenate(dfinal, 0)
    dout = r2 * (dfinal - out * (r2 * r2) * jnp.mean(dfinal * out, -1, keepdims=True))
    dmixed = dot_nt(dout.astype(BF16), wt[3])
    dprod = jnp.concatenate([at(dmixed, i) * at(v, j) for i, j in pairs], 0)
    dweights = dot_nn(dprod.astype(BF16), gather_heads)
    dweight = {pair: at(dweights, number) for number, pair in enumerate(pairs)}
    dscore = []
    for i in range(1, 4):
        mean = functools.reduce(jnp.add, [weight[i, j] * dweight[i, j] for j in range(i + 1)])
        for j in range(i + 1):
            dscore.append(weight[i, j] * (dweight[i, j] - mean) * 0.125)
    spread = dot_nn(jnp.concatenate(dscore, 0).astype(BF16), spread_heads)
    dwide = {pair: at(spread, number) for number, pair in enumerate(pairs)}
    add = lambda terms: functools.reduce(jnp.add, terms)
    dq = [add([dwide[i, j] * at(k, j) for j in range(i + 1)]) for i in range(1, 4)]
    dq = jnp.concatenate([jnp.zeros((n, 1024), F32)] + dq, 0)
    dk = jnp.concatenate([add([dwide[i, j] * at(q, i) for i in range(max(j, 1), 4)]) for j in range(4)], 0)
    dv = [add([wide[i, j] * at(dmixed, i) for i in range(max(j, 1), 4)]) for j in range(4)]
    dv = jnp.concatenate([dv[0] + at(dmixed, 0)] + dv[1:], 0)
    dnormed = dot_nt(dq.astype(BF16), wt[0]) + dot_nt(dk.astype(BF16), wt[1]) + dot_nt(dv.astype(BF16), wt[2])
    dstream = dout + r1 * (dnormed - stream * (r1 * r1) * jnp.mean(dnormed * stream, -1, keepdims=True))
    dctx_ref[...] = add([at(dstream, i) for i in range(4)]).astype(BF16)


def grad_body(rows_ref, cw_ref, out_ref):
    out_ref[...] = dot_nt(rows_ref[...], cw_ref[...]).astype(BF16)


def per_device(hidden_in, queries, keys, values, out_weight, context_weight, codes, table, depth_weights):
    c = lax.axis_index("c")

    keep, send, cw_cols = call(
        split_rows_body, (shape(8, 128, 384), shape(4, 128, 384), shape(1024, 256)), [ANY] * 4,
        queries, keys, values, context_weight,
        scratch=[pltpu.VMEM((3, 256, 512), BF16), pltpu.SemaphoreType.DMA((4,))], limit=60, nbytes=3 << 20,
    )
    full = lax.dynamic_update_slice(keep, move(send, other_core), ((1 - c) * 4, 0, 0))
    mine = lax.all_to_all(full, ("h", "z"), 0, 0, tiled=True)

    cw_l = move(cw_cols, l_swap)
    cw_c = move(cw_cols, other_core)
    cw_lc = move(cw_l, other_core)
    h_own, h_send = call(
        hidden_part_body, (shape(128, 1024, dtype=F32), shape(128, 1024)), [VM] * 2,
        hidden_in, context_weight, scratch=[pltpu.VMEM((256, 1024), F32)], flops=1 << 29, nbytes=3 << 20,
    )
    merged = call(
        merged_weight_body, shape(512, 256), [VM] * 5, out_weight, cw_cols, cw_c, cw_l, cw_lc,
        flops=1 << 30, nbytes=6 << 20,
    )
    half = shape(4, 128, 256)
    low, high, q = call(
        take_rows_body, (half, half, shape(8, 128, 128)), [VM], mine, after=(h_own, merged), nbytes=1 << 20
    )
    up_lo, down_hi = move(low, x_up), move(high, x_down)
    q_o = move(q, other_core)
    stats = (shape(128, 2048, dtype=F32), shape(1, 2048, dtype=F32), shape(1, 2048, dtype=F32))
    *carry, merged = call(
        own_block_body, stats + (shape(512, 256),), [VM] * 5, q, q_o, low, high, merged, flops=4 << 30, nbytes=2 << 20
    )
    pieces = [merged] + [move(merged, z_by(n)) for n in (1, 2, 3)]
    relay_lo, relay_hi = call(relay_body, (half, half), [VM] * 2, up_lo, down_hi, after=carry[1:2], nbytes=1 << 20)
    far_lo, far_hi = move(relay_lo, x_up), move(relay_hi, x_down)
    *carry, low, high = call(
        first_blocks_body, stats + (half, half), [VM] * 9, q, q_o, up_lo, down_hi, low, high, *carry, after=(relay_lo,),
        aliases={6: 0, 7: 1, 8: 2}, flops=3 << 30, nbytes=4 << 20,
    )
    up_hi, down_lo = move(high, x_up), move(low, x_down)
    carry = call(
        far_blocks_body, stats, [VM] * 7, q, q_o, far_lo, far_hi, *carry,
        aliases={4: 0, 5: 1, 6: 2}, flops=3 << 30, nbytes=3 << 20,
    )
    h_recv = move(h_send, other_core)
    embedded = call(embed_body, shape(3, 64, 1024), [VM] * 2, codes, table, after=carry[1:2], flops=3 << 27, nbytes=8 << 20)
    own, send, own_stat = call(
        last_blocks_body, (shape(128, 1024, dtype=F32), shape(160, 1024), shape(8, 1024, dtype=F32)),
        [VM] * 7, q, q_o, up_hi, down_lo, *carry, after=(embedded, h_recv, *pieces[1:]),
        scratch=[pltpu.VMEM(s.shape, s.dtype) for s in stats], flops=3 << 30, nbytes=3 << 20,
    )
    joined = move(send, other_core)
    attended = call(join_cores_body, shape(8, 128, 128), [VM] * 3, own, joined, own_stat, nbytes=1 << 20)
    merged = call(pack_body, shape(4, 512, 256), [VM] * 4, *pieces, after=(joined,), nbytes=2 << 20)
    merged_o = move(merged, other_core)
    attended = lax.all_to_all(attended, ("h", "z"), 0, 0, tiled=True)

    own, send = call(
        project_body, (shape(64, 1024, dtype=F32), shape(64, 1024)), [VM] * 5,
        attended, merged, merged_o, h_own, h_recv,
        scratch=[pltpu.VMEM((128, 1024), F32)], flops=1 << 28, nbytes=3 << 20,
    )
    recv = move(send, l_swap)
    losses, dcontext = call(
        depth_body, (shape(1, 64, dtype=F32), shape(64, 1024)), [VM] * 4 + [ANY] * 2,
        own, recv, embedded, codes, depth_weights, table,
        scratch=[pltpu.VMEM((4, 1024, 1024), BF16), pltpu.VMEM((4, 1024, 1024), BF16), pltpu.SemaphoreType.DMA((8,))],
        limit=60, flops=12 << 30, nbytes=17 << 20,
    )
    rows = lax.all_gather(dcontext, ("l", "c"), axis=0, tiled=True)
    grad = call(grad_body, shape(256, 1024), [VM] * 2, rows, context_weight, flops=1 << 29, nbytes=3 << 20)
    return losses.reshape(64), grad


def solution(mesh):
    fine = Mesh(mesh.devices.reshape(SIZES), AXES)
    seq, tp = AXES[:3], AXES[3:]
    return jax.shard_map(
        per_device,
        mesh=fine,
        in_specs=(
            P(seq, tp), P(seq, tp), P(seq, tp), P(seq, tp), P(tp, None), P(tp, None), P(seq + tp, None), P(), P(),
        ),
        out_specs=(P(seq + tp), P(seq, tp)),
        check_vma=False,
    )
```
